32 devices in a mesh: scen: 4 (over y, core), tm: 8 (over z, x).
Axes of the slice: x: 2, y: 2, z: 4, core: 2. Of those that a mesh axis runs over, the one named last changes fastest.
Arguments:
- cotangent: float32 [16, 336, 1024], P('scen', 'tm'), may hold values from -6 to 6
- blocks: bfloat16 [8, 6, 128, 128], P('tm'), may hold values from -0.21875 to 0.21875
- zone_links: int32 [8, 6], replicated, may hold values from 0 to 7, as said below
- step_size: float32 [1024], replicated, may hold values from 0.3 to 1
- coupling: bfloat16 [8, 336, 336], P('tm'), may hold values from -0.3125 to 0.3125
- ramp_band: int32 [8], P('tm'), may hold values from 42 to 336, as said below
- candidates: int32 [512], P('scen'), may hold values from 0 to 1023, as said below
Outputs:
- initial_adjoint: float32 [16, 336, 1024], P('scen', 'tm')
- siting_gradient: float32 [336, 512], P('tm', 'scen')
The draws below stay inside these ranges and needn't reach their ends.
Inputs may be any that keep to these rules, and one draw needn't show every extreme that they name: zone_links[z, 0] = z, and the 6 entries of a row are distinct zones. `ramp_band`: at least one zone has reach 336. `candidates`: the entries of block m of 128 consecutive entries are distinct buses in m * (256) to (m + 1) * 256 - 1.
All inputs are finite; a program needn't handle non-finite values.
Results may differ from the reference program's by a relative error of at most 0.0029.
Values may be sent and summed in bfloat16 or wider, within the bound.
A program may use at most 64 MiB of HBM per device.

```python
import math
import jax
import jax.numpy as jnp
from jax import lax

BUS = 128
HOURS = 336
NBR = 6
SWEEPS = 2
CAND_DEV = 128
ZONES = 8
NB = 1024
SCENS = 16
CANDS = 512


def draw_zone_links(key, part):
    keys = jax.random.split(key, ZONES)
    others = jax.vmap(lambda k: jax.random.permutation(k, ZONES - 1)[:NBR - 1])(keys)
    zone_ids = jnp.arange(ZONES, dtype=jnp.int32)
    rest = (zone_ids[:, None] + 1 + others.astype(jnp.int32)) % ZONES
    return jnp.concatenate([zone_ids[:, None], rest], axis=1).astype(jnp.int32)


def draw_ramp_band(key, part):
    first, second = jax.random.split(key)
    band = jax.random.randint(first, (ZONES,), HOURS // 8, HOURS + 1).astype(jnp.int32)
    widest = jax.random.randint(second, (), 0, ZONES)
    return band.at[widest].set(HOURS).astype(jnp.int32)


def draw_candidates(key, part):
    groups = CANDS // CAND_DEV
    width = NB // groups
    keys = jax.random.split(key, groups)
    chosen = jax.vmap(lambda k: jax.random.permutation(k, width)[:CAND_DEV])(keys).astype(jnp.int32)
    offsets = (jnp.arange(groups, dtype=jnp.int32) * width)[:, None]
    return (chosen + offsets).reshape(CANDS).astype(jnp.int32)


def strengthened(values, key, source, target, blocks, factor):
    def block_of(dim):
        return (jnp.arange(values.shape[dim]) // (values.shape[dim] // blocks)).reshape((-1,) + (1,) * (values.ndim - 1 - dim))

    one_side = jax.random.permutation(key, blocks)[block_of(target)]
    second = (block_of(target) + blocks // 2) % blocks
    return jnp.where((block_of(source) == one_side) | (block_of(source) == second), factor * values, values)


def steps_of(stream_key, extent, cuts, smallest, top_value):
    gain = 1.0
    for axis_at, blocks in cuts:
        heights = jax.random.uniform(jax.random.fold_in(jax.random.fold_in(stream_key, 6), axis_at), (blocks,), jnp.float32, smallest / len(cuts), top_value / len(cuts))
        gain = gain * jnp.repeat(jnp.exp(heights), extent[axis_at] // blocks).reshape((-1,) + (1,) * (len(extent) - 1 - axis_at))
    return gain


def centred(rng, extent, scale, bound, cuts=(), held_as=jnp.bfloat16):
    values = jax.random.normal(rng, extent, jnp.float32) * scale
    if len(cuts) > 0:
        values = steps_of(rng, extent, cuts, -0.22, 0.18) * values
    return jnp.clip(values, min=-bound, max=bound).astype(held_as)


def gaussian_with(own_key, shape, scale, reach, pieces, heavy, kind=jnp.bfloat16):
    values = scale * jax.random.normal(own_key, shape, jnp.float32)
    if pieces:
        values = values * steps_of(own_key, shape, pieces, -0.22, 0.18)
    return jnp.clip(strengthened(values, jax.random.fold_in(own_key, 3), *heavy), -reach, reach).astype(kind)


def setup_inputs(seed: int = 0) -> dict:
    arg_keys = jax.random.split(jax.random.key(seed), 8)
    cotangent = gaussian_with(arg_keys[0], (SCENS, HOURS, NB), 1.0, 6.0, ((0, 4), (1, 8)), (0, 2, 4, 2.0), jnp.float32)
    blocks = centred(arg_keys[1], (ZONES, NBR, BUS, BUS), (NBR * BUS) ** -0.5, 0.21875, ((0, 8),))
    zone_links = draw_zone_links(jax.random.fold_in(arg_keys[7], 71), 0)
    step_size = jnp.clip(jnp.exp(jax.random.uniform(arg_keys[3], (NB,), jnp.float32, math.log(0.3), math.log(1.0))), 0.3, 1.0)
    coupling = centred(arg_keys[4], (ZONES, HOURS, HOURS), HOURS ** -0.5, 0.3125, ((0, 8),))
    ramp_band = draw_ramp_band(jax.random.fold_in(arg_keys[7], 71), 0)
    candidates = draw_candidates(jax.random.fold_in(arg_keys[7], 71), 0)
    return dict(cotangent=cotangent, blocks=blocks, zone_links=zone_links, step_size=step_size, coupling=coupling, ramp_band=ramp_band, candidates=candidates)


def reference(cotangent, blocks, zone_links, step_size, coupling, ramp_band, candidates):
    hour_ids = jnp.arange(HOURS, dtype=jnp.int32)
    spread = jnp.abs(hour_ids[:, None] - hour_ids[None, :])
    masked = jnp.where(spread[None, :, :] <= ramp_band[:, None, None], coupling, jnp.zeros_like(coupling))
    blocks_wide = blocks.astype(jnp.float32)
    masked_wide = masked.astype(jnp.float32)

    def one_scenario(adjoint):
        grad_part = jnp.zeros((HOURS, NB), jnp.float32)
        for sweep in range(SWEEPS):
            weighted = adjoint * step_size[None, :]
            grad_part = grad_part + weighted
            scaled = weighted.astype(jnp.bfloat16)
            panel = scaled.astype(jnp.float32).reshape(HOURS, ZONES, BUS)
            picked = panel[:, zone_links, :]
            network = jnp.einsum("tzki,zkij->tzj", picked, blocks_wide).reshape(HOURS, NB)
            temporal = jnp.einsum("ztu,tzi->uzi", masked_wide, panel).reshape(HOURS, NB)
            temporal = temporal.astype(jnp.bfloat16).astype(jnp.float32)
            adjoint = adjoint - network - temporal
        return adjoint, grad_part

    def step_fn(total, adjoint):
        result, grad_part = one_scenario(adjoint)
        return total + grad_part, result

    total, initial_adjoint = lax.scan(step_fn, jnp.zeros((HOURS, NB), jnp.float32), cotangent)
    grad = total * (1.0 / SCENS)
    siting_gradient = grad[:, candidates]
    return initial_adjoint, siting_gradient
```

```python
import functools

import jax
import jax.numpy as jnp
from jax import lax
from jax.experimental import pallas as pl
from jax.experimental.pallas import tpu as pltpu
from jax.sharding import PartitionSpec as P

SWEEPS = 2
MESH = pl.DeviceIdType.MESH
F32 = jnp.float32
BF16 = jnp.bfloat16


def padded_coupling(coupling, band, slots, hours, padded):
    total = slots * hours
    rows = lax.broadcasted_iota(jnp.int32, (total, total), 0)
    cols = lax.broadcasted_iota(jnp.int32, (total, total), 1)
    masked = jnp.where(jnp.abs(rows - cols) <= band, coupling.astype(F32), 0.0).astype(BF16)
    wide = lax.broadcasted_iota(jnp.int32, (slots * padded, 1), 0)
    slot = jnp.zeros_like(wide)
    for j in range(1, slots):
        slot = slot + (wide >= j * padded).astype(jnp.int32)
    within = wide - slot * padded
    hour = jnp.where(within < hours, slot * hours + within, -1)
    place = lax.broadcasted_iota(jnp.int32, (slots * padded, total), 1)
    pick = jnp.where(hour == place, 1.0, 0.0).astype(BF16)
    both_last = (((1,), (1,)), ((), ()))
    turned = lax.dot_general(pick, masked, both_last, preferred_element_type=F32).astype(BF16)
    return lax.dot_general(turned, pick, both_last, preferred_element_type=F32).astype(BF16)


def kernel(
    tms, scs,
    cot_ref, blk_ref, links_ref, step_ref, coup_ref, band_ref, cand_ref,
    out_ref, sit_ref,
    adj, sbuf, recv, tsend, trecv, wall, turned, gacc, grecv,
    s_send, s_recv, t_send, t_recv, w1_send, w1_recv, w2_send, w2_recv, w3_send, w3_recv,
    g_send, g_recv,
):
    me = lax.axis_index("tm")
    mine = lax.axis_index("scen")
    scens, hours, _ = cot_ref.shape
    zones, _, padded, bus = adj.shape
    parts = wall.shape[0]
    fan = links_ref.shape[1]
    share = zones // scs

    barrier = pltpu.get_barrier_semaphore()
    for o in range(1, tms):
        pl.semaphore_signal(barrier, inc=1, device_id={"tm": lax.rem(me + o, tms)}, device_id_type=MESH)
    for o in range(1, scs):
        pl.semaphore_signal(barrier, inc=1, device_id={"scen": lax.rem(mine + o, scs)}, device_id_type=MESH)

    def to_tm(src, dst, send, got, o):
        return pltpu.make_async_remote_copy(
            src_ref=src, dst_ref=dst, send_sem=send, recv_sem=got,
            device_id={"tm": lax.rem(me + o, tms)}, device_id_type=MESH,
        )

    def to_scen(src, dst, send, got, peer):
        return pltpu.make_async_remote_copy(
            src_ref=src, dst_ref=dst, send_sem=send, recv_sem=got,
            device_id={"scen": peer}, device_id_type=MESH,
        )

    def scale(sweep, z):
        weighted = adj[z] * step_ref[z][None]
        sbuf[sweep, z] = weighted.astype(BF16)
        part = jnp.sum(weighted, axis=0) * (1.0 / (scens * scs))
        gacc[z] = part if sweep == 0 else gacc[z] + part

    def send_scaled(sweep, o):
        copy = to_tm(
            sbuf.at[sweep, lax.rem(me + o, tms)], recv.at[sweep, me],
            s_send.at[sweep, o], s_recv.at[sweep, o], o,
        )
        copy.start()
        return copy

    def temporal(sweep):
        side = jnp.concatenate(
            [recv[sweep, :, s].reshape(tms * padded, bus) for s in range(scens)], axis=1
        )
        for j in range(tms):
            rows = turned[j * padded:(j + 1) * padded, :]
            term = jnp.dot(rows, side, preferred_element_type=F32).astype(BF16)
            for s in range(scens):
                tsend[sweep, j, s] = term[:, s * bus:(s + 1) * bus]
        copies = []
        for o in range(1, tms):
            copy = to_tm(
                tsend.at[sweep, lax.rem(me + o, tms)], trecv.at[sweep, me],
                t_send.at[sweep, o], t_recv.at[sweep, o], o,
            )
            copy.start()
            copies.append(copy)
        trecv[sweep, me] = tsend[sweep, me]
        return copies

    def network(sweep):
        def one(z, _):
            picked = jnp.concatenate(
                [sbuf[sweep, links_ref[z, k]].reshape(scens * padded, bus) for k in range(fan)], axis=1
            )
            weights = jnp.concatenate([wall[p, z] for p in range(parts)], axis=0)
            term = jnp.dot(picked, weights, preferred_element_type=F32)
            adj[z] = adj[z] - term.reshape(scens, padded, bus)
            return 0

        lax.fori_loop(0, zones, one, 0)

    adj[...] = jnp.zeros_like(adj)
    for s in range(scens):
        for z in range(zones):
            adj[z, s, 0:hours, :] = cot_ref[s, :, z * bus:(z + 1) * bus]

    def first(z, _):
        scale(0, z)
        return 0

    lax.fori_loop(0, zones, first, 0)
    wall[mine, me] = blk_ref[mine]
    pl.semaphore_wait(barrier, tms - 1 + scs - 1)

    sent = []
    scaled_out = [send_scaled(0, o) for o in range(1, tms)]
    recv[0, me] = sbuf[0, me]
    first_leg = []
    for o in range(1, tms):
        copy = to_tm(wall.at[mine, me], wall.at[mine, me], w1_send.at[o], w1_recv.at[o], o)
        copy.start()
        first_leg.append(copy)
    turned[...] = padded_coupling(coup_ref[...], band_ref[0], tms, hours, padded)

    for copy in scaled_out:
        copy.wait_recv()
    temporal_out = temporal(0)
    sent += scaled_out + temporal_out

    for copy in first_leg:
        copy.wait_recv()
    core = lax.rem(mine, 2)
    other = mine + 1 - 2 * core
    second_leg = []
    third_leg = []
    for o in range(1, scs // 2):
        copy = to_scen(
            wall.at[mine], wall.at[mine], w2_send.at[o], w2_recv.at[o], lax.rem(mine + 2 * o, scs)
        )
        copy.start()
        second_leg.append(copy)
    for o in range(scs // 2):
        if o > 0:
            second_leg[o - 1].wait_recv()
        part = lax.rem(mine + scs - 2 * o, scs)
        copy = to_scen(wall.at[part], wall.at[part], w3_send.at[o], w3_recv.at[o], other)
        copy.start()
        third_leg.append(copy)
    for copy in third_leg:
        copy.wait_recv()
    sent += first_leg + second_leg + third_leg

    network(0)
    scaled_out = []
    for o in range(tms):
        zone = lax.rem(me + o, tms)
        if o > 0:
            temporal_out[tms - o - 1].wait_recv()
        adj[zone] = adj[zone] - trecv[0, zone].astype(F32)
        scale(1, zone)
        if o > 0:
            scaled_out.append(send_scaled(1, o))
    recv[1, me] = sbuf[1, me]

    grads = []
    for o in range(1, scs):
        peer = lax.rem(mine + o, scs)
        copy = to_scen(gacc.at[pl.ds(peer * share, share)], grecv.at[o], g_send.at[o], g_recv.at[o], peer)
        copy.start()
        grads.append(copy)

    network(1)
    for copy in scaled_out:
        copy.wait_recv()
    temporal_out = temporal(1)
    sent += scaled_out + temporal_out + grads

    for copy in grads:
        copy.wait_recv()
    total = gacc[pl.ds(mine * share, share)]
    for o in range(1, scs):
        total = total + grecv[o]
    local = cand_ref[...] - mine * (share * bus)
    siting = jnp.zeros((padded, cand_ref.shape[1]), F32)
    for part in range(share):
        ids = lax.broadcasted_iota(jnp.int32, (bus, cand_ref.shape[1]), 0) + part * bus
        chosen = jnp.where(ids == local, 1.0, 0.0)
        siting = siting + jnp.dot(
            total[part], chosen, preferred_element_type=F32, precision=lax.Precision.HIGHEST
        )
    sit_ref[...] = siting[0:hours]

    for copy in temporal_out:
        copy.wait_recv()
    for z in range(zones):
        for s in range(scens):
            value = adj[z, s] - trecv[1, z, s].astype(F32)
            out_ref[s, :, z * bus:(z + 1) * bus] = value[0:hours]
    for copy in sent:
        copy.wait_send()


def per_device(tms, scs, cotangent, blocks, zone_links, step_size, coupling, ramp_band, candidates):
    scens, hours, buses = cotangent.shape
    _, fan, bus, _ = blocks.shape
    zones = buses // bus
    padded = -(-hours // 16) * 16
    rows = fan * bus // scs
    vmem = pl.BlockSpec(memory_space=pltpu.VMEM)
    smem = pl.BlockSpec(memory_space=pltpu.SMEM)
    dma = pltpu.SemaphoreType.DMA
    return pl.pallas_call(
        functools.partial(kernel, tms, scs),
        out_shape=(
            jax.ShapeDtypeStruct(cotangent.shape, F32),
            jax.ShapeDtypeStruct((hours, candidates.shape[0]), F32),
        ),
        in_specs=[vmem, vmem, smem, vmem, vmem, smem, vmem],
        out_specs=(vmem, vmem),
        scratch_shapes=[
            pltpu.VMEM((zones, scens, padded, bus), F32),
            pltpu.VMEM((SWEEPS, zones, scens, padded, bus), BF16),
            pltpu.VMEM((SWEEPS, tms, scens, padded, bus), BF16),
            pltpu.VMEM((SWEEPS, tms, scens, padded, bus), BF16),
            pltpu.VMEM((SWEEPS, zones, scens, padded, bus), BF16),
            pltpu.VMEM((scs, zones, rows, bus), BF16),
            pltpu.VMEM((tms * padded, tms * padded), BF16),
            pltpu.VMEM((zones, padded, bus), F32),
            pltpu.VMEM((scs, zones // scs, padded, bus), F32),
            dma((SWEEPS, tms)), dma((SWEEPS, tms)), dma((SWEEPS, tms)), dma((SWEEPS, tms)),
            dma((tms,)), dma((tms,)), dma((scs,)), dma((scs,)), dma((scs,)), dma((scs,)),
            dma((scs,)), dma((scs,)),
        ],
        compiler_params=pltpu.CompilerParams(
            collective_id=0, has_side_effects=True, vmem_limit_bytes=40 * 1024 * 1024
        ),
        name="sweeps",
    )(
        cotangent,
        blocks.reshape(scs, rows, bus),
        zone_links,
        step_size.reshape(zones, 1, bus),
        coupling.reshape(coupling.shape[1:]),
        ramp_band,
        candidates.reshape(1, -1),
    )


def solution(mesh):
    placed = (
        P("scen", "tm", None),
        P("tm", None, None, None),
        P(),
        P(),
        P("tm", None, None),
        P("tm"),
        P("scen"),
    )
    return jax.shard_map(
        functools.partial(per_device, mesh.shape["tm"], mesh.shape["scen"]),
        mesh=mesh,
        in_specs=placed,
        out_specs=(P("scen", "tm", None), P("tm", "scen")),
        check_vma=False,
    )
```

```python
import functools

import jax
import jax.numpy as jnp
from jax import lax
from jax.experimental import pallas as pl
from jax.experimental.pallas import tpu as pltpu
from jax.sharding import PartitionSpec as P

SWEEPS = 2
MESH = pl.DeviceIdType.MESH
F32 = jnp.float32
BF16 = jnp.bfloat16


def kernel(
    tms, scs,
    cot_ref, blk_ref, links_ref, step_ref, coup_ref, band_ref, cand_ref,
    out_ref, sit_ref,
    adj, sbuf, recv, tsend, trecv, wall, pick, turned, gacc, gsum, grecv,
    s_send, s_recv, t_send, t_recv, wz_send, wz_recv, wx_send, wx_recv, wy_send, wy_recv,
    wc_send, wc_recv, g_send, g_recv,
):
    me = lax.axis_index("tm")
    mine = lax.axis_index("scen")
    hours, scens, _ = cot_ref.shape
    zones, rows, bus = adj.shape
    parts, width, depth = wall.shape[:3]
    fan = links_ref.shape[1]
    share = zones // scs
    used = hours * scens
    total = tms * hours
    padded = gsum.shape[1]
    col = lax.rem(me, width)
    plane = lax.div(me, width)
    far_first = sorted(range(1, tms), key=lambda o: abs(2 * o - tms))
    both_last = (((1,), (1,)), ((), ()))

    barrier = pltpu.get_barrier_semaphore()
    for o in range(1, tms):
        pl.semaphore_signal(barrier, inc=1, device_id={"tm": lax.rem(me + o, tms)}, device_id_type=MESH)
    for o in range(1, scs):
        pl.semaphore_signal(barrier, inc=1, device_id={"scen": lax.rem(mine + o, scs)}, device_id_type=MESH)

    def remote(src, dst, send, got, axis, peer):
        copy = pltpu.make_async_remote_copy(
            src_ref=src, dst_ref=dst, send_sem=send, recv_sem=got,
            device_id={axis: peer}, device_id_type=MESH,
        )
        copy.start()
        return copy

    def scale(sweep, z):
        weighted = adj[z] * step_ref[z]
        sbuf[sweep, z] = weighted.astype(BF16)
        gacc[z] = weighted if sweep == 0 else gacc[z] + weighted

    def send_scaled(sweep, o):
        to = lax.rem(me + o, tms)
        return remote(
            sbuf.at[sweep, to], recv.at[sweep, me], s_send.at[sweep, o], s_recv.at[sweep, o], "tm", to
        )

    def temporal(sweep):
        side = recv[sweep].reshape(tms * rows, bus)
        copies = {}
        for o in far_first:
            to = lax.rem(me + o, tms)
            tsend[sweep, to] = jnp.dot(turned[to], side, preferred_element_type=F32).astype(BF16)
            copies[o] = remote(
                tsend.at[sweep, to], trecv.at[sweep, me], t_send.at[sweep, o], t_recv.at[sweep, o], "tm", to
            )
        trecv[sweep, me] = jnp.dot(turned[me], side, preferred_element_type=F32).astype(BF16)
        return copies

    def network(sweep):
        def one(z, _):
            picked = jnp.concatenate([sbuf[sweep, links_ref[z, k]] for k in range(fan)], axis=1)
            weights = jnp.concatenate(
                [wall[p, lax.rem(z, width), lax.div(z, width)] for p in range(parts)], axis=0
            )
            adj[z] = adj[z] - jnp.dot(picked, weights, preferred_element_type=F32)
            return 0

        lax.fori_loop(0, zones, one, 0, unroll=2)

    for z in range(zones):
        adj[z, used // 16 * 16:rows, :] = jnp.zeros((rows - used // 16 * 16, bus), F32)
        adj[z, 0:used, :] = cot_ref[:, :, z * bus:(z + 1) * bus].reshape(used, bus)
        scale(0, z)
    wall[mine, col, plane] = blk_ref[mine]
    pl.semaphore_wait(barrier, tms - 1 + scs - 1)

    along_z = []
    for o in range(1, depth):
        to = lax.rem(plane + o, depth) * width + col
        piece = wall.at[mine, col, plane]
        along_z.append(remote(piece, piece, wz_send.at[o], wz_recv.at[o], "tm", to))
    scaled_out = {o: send_scaled(0, o) for o in far_first}
    recv[0, me] = sbuf[0, me]

    spread = lax.broadcasted_iota(jnp.int32, (total, total), 0) - lax.broadcasted_iota(jnp.int32, (total, total), 1)
    masked = jnp.where(jnp.abs(spread) <= band_ref[0], coup_ref[...].astype(F32), 0.0).astype(BF16)
    at_row = lax.broadcasted_iota(jnp.int32, (rows, total), 0)
    ahead = at_row - scens * lax.broadcasted_iota(jnp.int32, (rows, total), 1)
    for j in range(tms):
        over = ahead + j * used
        pick[j] = jnp.where((over >= 0) & (over < scens) & (at_row < used), 1.0, 0.0).astype(BF16)

    def turn(j, _):
        half = lax.dot_general(pick[j], masked, both_last, preferred_element_type=F32).astype(BF16)
        whole = lax.dot_general(
            half, pick[...].reshape(tms * rows, total), both_last, preferred_element_type=F32
        )
        one = lax.broadcasted_iota(jnp.int32, (rows, tms * rows), 0)
        two = lax.broadcasted_iota(jnp.int32, (rows, tms * rows), 1)
        same = jnp.bitwise_and(one - two, scens - 1) == 0
        turned[j] = jnp.where(same, whole, 0.0).astype(BF16)
        return 0

    lax.fori_loop(0, tms, turn, 0)

    core = lax.rem(mine, 2)
    along_y = {}

    def to_same_core(back):
        held = lax.rem(col + width - back, width)
        for o in range(1, scs // 2):
            piece = wall.at[mine, held]
            along_y[o, back] = remote(
                piece, piece, wy_send.at[o, back], wy_recv.at[o, back], "scen", lax.rem(mine + 2 * o, scs)
            )

    for copy in along_z:
        copy.wait_recv()
    along_x = []
    for o in range(1, width):
        piece = wall.at[mine, col]
        to = plane * width + lax.rem(col + o, width)
        along_x.append(remote(piece, piece, wx_send.at[o], wx_recv.at[o], "tm", to))
    to_same_core(0)
    for o in range(1, width):
        along_x[o - 1].wait_recv()
        to_same_core(o)

    for o in far_first:
        scaled_out[o].wait_recv()
    temporal_out = temporal(0)
    sent = along_z + along_x + list(along_y.values()) + list(scaled_out.values()) + list(temporal_out.values())

    to_core = []
    for o in range(scs // 2):
        if o > 0:
            for back in range(width):
                along_y[o, back].wait_recv()
        piece = wall.at[lax.rem(mine + scs - 2 * o, scs)]
        to_core.append(remote(piece, piece, wc_send.at[o], wc_recv.at[o], "scen", mine + 1 - 2 * core))
    for copy in to_core:
        copy.wait_recv()
    sent += to_core

    network(0)
    scaled_out = {}
    for o in far_first:
        zone = lax.rem(me + o, tms)
        temporal_out[tms - o].wait_recv()
        adj[zone] = adj[zone] - trecv[0, zone].astype(F32)
        scale(1, zone)
        scaled_out[o] = send_scaled(1, o)
    adj[me] = adj[me] - trecv[0, me].astype(F32)
    scale(1, me)
    recv[1, me] = sbuf[1, me]

    network(1)

    hour_of = lax.broadcasted_iota(jnp.int32, (padded, rows), 1) - scens * lax.broadcasted_iota(
        jnp.int32, (padded, rows), 0
    )
    fold = jnp.where((hour_of >= 0) & (hour_of < scens), 1.0 / (scens * scs), 0.0)

    def fold_zone(z, _):
        gsum[z] = jnp.dot(fold, gacc[z], preferred_element_type=F32, precision=lax.Precision.HIGHEST)
        return 0

    lax.fori_loop(0, zones, fold_zone, 0)
    grads = []
    for o in range(1, scs):
        peer = lax.rem(mine + o, scs)
        grads.append(remote(
            gsum.at[pl.ds(peer * share, share)], grecv.at[o], g_send.at[o], g_recv.at[o], "scen", peer
        ))

    for o in far_first:
        scaled_out[o].wait_recv()
    temporal_out = temporal(1)
    sent += list(scaled_out.values()) + list(temporal_out.values()) + grads

    for copy in grads:
        copy.wait_recv()
    summed = gsum[pl.ds(mine * share, share)]
    for o in range(1, scs):
        summed = summed + grecv[o]
    local = cand_ref[...] - mine * (share * bus)
    siting = jnp.zeros((padded, cand_ref.shape[1]), F32)
    for part in range(share):
        ids = lax.broadcasted_iota(jnp.int32, (bus, cand_ref.shape[1]), 0) + part * bus
        chosen = jnp.where(ids == local, 1.0, 0.0)
        siting = siting + jnp.dot(
            summed[part], chosen, preferred_element_type=F32, precision=lax.Precision.HIGHEST
        )
    sit_ref[...] = siting[0:hours]

    def finish(zone):
        value = adj[zone] - trecv[1, zone].astype(F32)
        lanes = pl.ds(pl.multiple_of(zone * bus, bus), bus)
        out_ref[:, :, lanes] = value[0:used].reshape(hours, scens, bus)

    finish(me)
    for o in far_first:
        temporal_out[tms - o].wait_recv()
        finish(lax.rem(me + o, tms))
    for copy in sent:
        copy.wait_send()


def per_device(tms, scs, cotangent, blocks, zone_links, step_size, coupling, ramp_band, candidates):
    scens, hours, buses = cotangent.shape
    _, fan, bus, _ = blocks.shape
    zones = buses // bus
    rows = -(-hours * scens // 16) * 16
    padded = -(-hours // 8) * 8
    cut = fan * bus // scs
    width = 1
    while 4 * width * width <= tms:
        width *= 2
    depth = tms // width
    vmem = pl.BlockSpec(memory_space=pltpu.VMEM)
    smem = pl.BlockSpec(memory_space=pltpu.SMEM)
    dma = pltpu.SemaphoreType.DMA
    adjoint, siting_gradient = pl.pallas_call(
        functools.partial(kernel, tms, scs),
        out_shape=(
            jax.ShapeDtypeStruct((hours, scens, buses), F32),
            jax.ShapeDtypeStruct((hours, candidates.shape[0]), F32),
        ),
        in_specs=[vmem, vmem, smem, vmem, vmem, smem, vmem],
        out_specs=(vmem, vmem),
        scratch_shapes=[
            pltpu.VMEM((zones, rows, bus), F32),
            pltpu.VMEM((SWEEPS, zones, rows, bus), BF16),
            pltpu.VMEM((SWEEPS, tms, rows, bus), BF16),
            pltpu.VMEM((SWEEPS, tms, rows, bus), BF16),
            pltpu.VMEM((SWEEPS, zones, rows, bus), BF16),
            pltpu.VMEM((scs, width, depth, cut, bus), BF16),
            pltpu.VMEM((tms, rows, tms * hours), BF16),
            pltpu.VMEM((tms, rows, tms * rows), BF16),
            pltpu.VMEM((zones, rows, bus), F32),
            pltpu.VMEM((zones, padded, bus), F32),
            pltpu.VMEM((scs, zones // scs, padded, bus), F32),
            dma((SWEEPS, tms)), dma((SWEEPS, tms)), dma((SWEEPS, tms)), dma((SWEEPS, tms)),
            dma((depth,)), dma((depth,)), dma((width,)), dma((width,)),
            dma((scs, width)), dma((scs, width)), dma((scs,)), dma((scs,)), dma((scs,)), dma((scs,)),
        ],
        compiler_params=pltpu.CompilerParams(
            collective_id=0, has_side_effects=True, vmem_limit_bytes=40 * 1024 * 1024
        ),
        name="sweeps",
    )(
        jnp.transpose(cotangent, (1, 0, 2)),
        blocks.reshape(scs, cut, bus),
        zone_links,
        step_size.reshape(zones, 1, bus),
        coupling.reshape(coupling.shape[1:]),
        ramp_band,
        candidates.reshape(1, -1),
    )
    return jnp.transpose(adjoint, (1, 0, 2)), siting_gradient


def solution(mesh):
    placed = (
        P("scen", "tm", None),
        P("tm", None, None, None),
        P(),
        P(),
        P("tm", None, None),
        P("tm"),
        P("scen"),
    )
    return jax.shard_map(
        functools.partial(per_device, mesh.shape["tm"], mesh.shape["scen"]),
        mesh=mesh,
        in_specs=placed,
        out_specs=(P("scen", "tm", None), P("tm", "scen")),
        check_vma=False,
    )
```

```python
import functools

import jax
import jax.numpy as jnp
from jax import lax
from jax.experimental import pallas as pl
from jax.experimental.pallas import tpu as pltpu
from jax.sharding import PartitionSpec as P

SWEEPS = 2
MESH = pl.DeviceIdType.MESH
F32 = jnp.float32
BF16 = jnp.bfloat16


def kernel(
    tms, scs,
    cot_hbm, blk_hbm, links_ref, step_hbm, coup_hbm, band_ref, cand_hbm,
    out_hbm, sit_hbm,
    cot_ref, step_ref, coup_ref, cand_ref, out_ref, sit_ref, in_sem, out_sem,
    adj, sbuf, recv, tsend, trecv, wall, pick, turned, gacc, gsum, grecv,
    s_send, s_recv, t_send, t_recv, wz_send, wz_recv, wx_send, wx_recv, wy_send, wy_recv,
    wc_send, wc_recv, g_send, g_recv,
):
    me = lax.axis_index("tm")
    mine = lax.axis_index("scen")
    hours, scens, _ = cot_ref.shape
    zones, rows, bus = adj.shape
    parts, width, depth = wall.shape[:3]
    fan = links_ref.shape[1]
    share = zones // scs
    used = hours * scens
    total = tms * hours
    padded = gsum.shape[1]
    col = lax.rem(me, width)
    plane = lax.div(me, width)
    far_first = sorted(range(1, tms), key=lambda o: abs(2 * o - tms))
    both_last = (((1,), (1,)), ((), ()))

    loads = [
        pltpu.make_async_copy(src, dst, in_sem.at[i])
        for i, (src, dst) in enumerate([
            (cot_hbm, cot_ref), (step_hbm, step_ref), (blk_hbm.at[mine], wall.at[mine, col, plane]),
            (coup_hbm, coup_ref), (cand_hbm, cand_ref),
        ])
    ]
    for load in loads:
        load.start()
    barrier = pltpu.get_barrier_semaphore()
    for o in range(1, tms):
        pl.semaphore_signal(barrier, inc=1, device_id={"tm": lax.rem(me + o, tms)}, device_id_type=MESH)
    for o in range(1, scs):
        pl.semaphore_signal(barrier, inc=1, device_id={"scen": lax.rem(mine + o, scs)}, device_id_type=MESH)

    def remote(src, dst, send, got, axis, peer):
        copy = pltpu.make_async_remote_copy(
            src_ref=src, dst_ref=dst, send_sem=send, recv_sem=got,
            device_id={axis: peer}, device_id_type=MESH,
        )
        copy.start()
        return copy

    def scale(sweep, z):
        weighted = adj[z] * step_ref[z]
        sbuf[sweep, z] = weighted.astype(BF16)
        gacc[z] = weighted if sweep == 0 else gacc[z] + weighted

    def send_scaled(sweep, o):
        to = lax.rem(me + o, tms)
        return remote(
            sbuf.at[sweep, to], recv.at[sweep, me], s_send.at[sweep, o], s_recv.at[sweep, o], "tm", to
        )

    def temporal(sweep):
        side = recv[sweep].reshape(tms * rows, bus)
        copies = {}
        for o in far_first:
            to = lax.rem(me + o, tms)
            tsend[sweep, to] = jnp.dot(turned[to], side, preferred_element_type=F32).astype(BF16)
            copies[o] = remote(
                tsend.at[sweep, to], trecv.at[sweep, me], t_send.at[sweep, o], t_recv.at[sweep, o], "tm", to
            )
        trecv[sweep, me] = jnp.dot(turned[me], side, preferred_element_type=F32).astype(BF16)
        return copies

    def network(sweep):
        def one(z, _):
            picked = jnp.concatenate([sbuf[sweep, links_ref[z, k]] for k in range(fan)], axis=1)
            weights = jnp.concatenate(
                [wall[p, lax.rem(z, width), lax.div(z, width)] for p in range(parts)], axis=0
            )
            adj[z] = adj[z] - jnp.dot(picked, weights, preferred_element_type=F32)
            return 0

        lax.fori_loop(0, zones, one, 0, unroll=2)

    loads[0].wait()
    loads[1].wait()
    for z in range(zones):
        adj[z, used // 16 * 16:rows, :] = jnp.zeros((rows - used // 16 * 16, bus), F32)
        adj[z, 0:used, :] = cot_ref[:, :, z * bus:(z + 1) * bus].reshape(used, bus)
        scale(0, z)
    loads[2].wait()
    pl.semaphore_wait(barrier, tms - 1 + scs - 1)

    along_z = []
    for o in range(1, depth):
        to = lax.rem(plane + o, depth) * width + col
        piece = wall.at[mine, col, plane]
        along_z.append(remote(piece, piece, wz_send.at[o], wz_recv.at[o], "tm", to))
    scaled_out = {o: send_scaled(0, o) for o in far_first}
    recv[0, me] = sbuf[0, me]

    loads[3].wait()
    loads[4].wait()
    spread = lax.broadcasted_iota(jnp.int32, (total, total), 0) - lax.broadcasted_iota(jnp.int32, (total, total), 1)
    masked = jnp.where(jnp.abs(spread) <= band_ref[0], coup_ref[...].astype(F32), 0.0).astype(BF16)
    at_row = lax.broadcasted_iota(jnp.int32, (rows, total), 0)
    ahead = at_row - scens * lax.broadcasted_iota(jnp.int32, (rows, total), 1)
    for j in range(tms):
        over = ahead + j * used
        pick[j] = jnp.where((over >= 0) & (over < scens) & (at_row < used), 1.0, 0.0).astype(BF16)

    def turn(j, _):
        half = lax.dot_general(pick[j], masked, both_last, preferred_element_type=F32).astype(BF16)
        whole = lax.dot_general(
            half, pick[...].reshape(tms * rows, total), both_last, preferred_element_type=F32
        )
        one = lax.broadcasted_iota(jnp.int32, (rows, tms * rows), 0)
        two = lax.broadcasted_iota(jnp.int32, (rows, tms * rows), 1)
        same = jnp.bitwise_and(one - two, scens - 1) == 0
        turned[j] = jnp.where(same, whole, 0.0).astype(BF16)
        return 0

    lax.fori_loop(0, tms, turn, 0)

    core = lax.rem(mine, 2)
    along_y = {}

    def to_same_core(back):
        held = lax.rem(col + width - back, width)
        for o in range(1, scs // 2):
            piece = wall.at[mine, held]
            along_y[o, back] = remote(
                piece, piece, wy_send.at[o, back], wy_recv.at[o, back], "scen", lax.rem(mine + 2 * o, scs)
            )

    for copy in along_z:
        copy.wait_recv()
    along_x = []
    for o in range(1, width):
        piece = wall.at[mine, col]
        to = plane * width + lax.rem(col + o, width)
        along_x.append(remote(piece, piece, wx_send.at[o], wx_recv.at[o], "tm", to))
    to_same_core(0)
    for o in range(1, width):
        along_x[o - 1].wait_recv()
        to_same_core(o)

    for o in far_first:
        scaled_out[o].wait_recv()
    temporal_out = temporal(0)
    sent = along_z + along_x + list(along_y.values()) + list(scaled_out.values()) + list(temporal_out.values())

    to_core = []
    for o in range(scs // 2):
        if o > 0:
            for back in range(width):
                along_y[o, back].wait_recv()
        piece = wall.at[lax.rem(mine + scs - 2 * o, scs)]
        to_core.append(remote(piece, piece, wc_send.at[o], wc_recv.at[o], "scen", mine + 1 - 2 * core))
    for copy in to_core:
        copy.wait_recv()
    sent += to_core

    network(0)
    scaled_out = {}
    for o in far_first:
        zone = lax.rem(me + o, tms)
        temporal_out[tms - o].wait_recv()
        adj[zone] = adj[zone] - trecv[0, zone].astype(F32)
        scale(1, zone)
        scaled_out[o] = send_scaled(1, o)
    adj[me] = adj[me] - trecv[0, me].astype(F32)
    scale(1, me)
    recv[1, me] = sbuf[1, me]

    network(1)

    hour_of = lax.broadcasted_iota(jnp.int32, (padded, rows), 1) - scens * lax.broadcasted_iota(
        jnp.int32, (padded, rows), 0
    )
    fold = jnp.where((hour_of >= 0) & (hour_of < scens), 1.0 / (scens * scs), 0.0)

    def fold_zone(z, _):
        gsum[z] = jnp.dot(fold, gacc[z], preferred_element_type=F32, precision=lax.Precision.HIGHEST)
        return 0

    lax.fori_loop(0, zones, fold_zone, 0)
    grads = []
    for o in range(1, scs):
        peer = lax.rem(mine + o, scs)
        grads.append(remote(
            gsum.at[pl.ds(peer * share, share)], grecv.at[o], g_send.at[o], g_recv.at[o], "scen", peer
        ))

    for o in far_first:
        scaled_out[o].wait_recv()
    temporal_out = temporal(1)
    sent += list(scaled_out.values()) + list(temporal_out.values()) + grads

    for copy in grads:
        copy.wait_recv()
    summed = gsum[pl.ds(mine * share, share)]
    for o in range(1, scs):
        summed = summed + grecv[o]
    local = cand_ref[...] - mine * (share * bus)
    siting = jnp.zeros((padded, cand_ref.shape[1]), F32)
    for part in range(share):
        ids = lax.broadcasted_iota(jnp.int32, (bus, cand_ref.shape[1]), 0) + part * bus
        chosen = jnp.where(ids == local, 1.0, 0.0)
        siting = siting + jnp.dot(
            summed[part], chosen, preferred_element_type=F32, precision=lax.Precision.HIGHEST
        )
    sit_ref[...] = siting[0:hours]
    stores = [pltpu.make_async_copy(sit_ref, sit_hbm, out_sem.at[0])]
    stores[0].start()

    def finish(zone, o):
        value = adj[zone] - trecv[1, zone].astype(F32)
        lanes = pl.ds(pl.multiple_of(zone * bus, bus), bus)
        out_ref[:, :, lanes] = value[0:used].reshape(hours, scens, bus)
        store = pltpu.make_async_copy(out_ref.at[:, :, lanes], out_hbm.at[:, :, lanes], out_sem.at[o + 1])
        store.start()
        stores.append(store)

    finish(me, 0)
    for o in far_first:
        temporal_out[tms - o].wait_recv()
        finish(lax.rem(me + o, tms), o)
    for copy in sent:
        copy.wait_send()
    for store in stores:
        store.wait()


def per_device(tms, scs, cotangent, blocks, zone_links, step_size, coupling, ramp_band, candidates):
    scens, hours, buses = cotangent.shape
    _, fan, bus, _ = blocks.shape
    zones = buses // bus
    rows = -(-hours * scens // 16) * 16
    padded = -(-hours // 8) * 8
    cut = fan * bus // scs
    width = 1
    while 4 * width * width <= tms:
        width *= 2
    depth = tms // width
    hbm = pl.BlockSpec(memory_space=pltpu.HBM)
    smem = pl.BlockSpec(memory_space=pltpu.SMEM)
    dma = pltpu.SemaphoreType.DMA
    adjoint, siting_gradient = pl.pallas_call(
        functools.partial(kernel, tms, scs),
        out_shape=(
            jax.ShapeDtypeStruct((hours, scens, buses), F32),
            jax.ShapeDtypeStruct((hours, candidates.shape[0]), F32),
        ),
        in_specs=[hbm, hbm, smem, hbm, hbm, smem, hbm],
        out_specs=(hbm, hbm),
        scratch_shapes=[
            pltpu.VMEM((hours, scens, buses), F32),
            pltpu.VMEM((zones, 1, bus), F32),
            pltpu.VMEM(coupling.shape[1:], BF16),
            pltpu.VMEM((1, candidates.shape[0]), jnp.int32),
            pltpu.VMEM((hours, scens, buses), F32),
            pltpu.VMEM((hours, candidates.shape[0]), F32),
            dma((5,)), dma((tms + 1,)),
            pltpu.VMEM((zones, rows, bus), F32),
            pltpu.VMEM((SWEEPS, zones, rows, bus), BF16),
            pltpu.VMEM((SWEEPS, tms, rows, bus), BF16),
            pltpu.VMEM((SWEEPS, tms, rows, bus), BF16),
            pltpu.VMEM((SWEEPS, zones, rows, bus), BF16),
            pltpu.VMEM((scs, width, depth, cut, bus), BF16),
            pltpu.VMEM((tms, rows, tms * hours), BF16),
            pltpu.VMEM((tms, rows, tms * rows), BF16),
            pltpu.VMEM((zones, rows, bus), F32),
            pltpu.VMEM((zones, padded, bus), F32),
            pltpu.VMEM((scs, zones // scs, padded, bus), F32),
            dma((SWEEPS, tms)), dma((SWEEPS, tms)), dma((SWEEPS, tms)), dma((SWEEPS, tms)),
            dma((depth,)), dma((depth,)), dma((width,)), dma((width,)),
            dma((scs, width)), dma((scs, width)), dma((scs,)), dma((scs,)), dma((scs,)), dma((scs,)),
        ],
        compiler_params=pltpu.CompilerParams(
            collective_id=0, has_side_effects=True, vmem_limit_bytes=62 * 1024 * 1024
        ),
        name="sweeps",
    )(
        jnp.transpose(cotangent, (1, 0, 2)),
        blocks.reshape(scs, cut, bus),
        zone_links,
        step_size.reshape(zones, 1, bus),
        coupling.reshape(coupling.shape[1:]),
        ramp_band,
        candidates.reshape(1, -1),
    )
    return jnp.transpose(adjoint, (1, 0, 2)), siting_gradient


def solution(mesh):
    placed = (
        P("scen", "tm", None),
        P("tm", None, None, None),
        P(),
        P(),
        P("tm", None, None),
        P("tm"),
        P("scen"),
    )
    return jax.shard_map(
        functools.partial(per_device, mesh.shape["tm"], mesh.shape["scen"]),
        mesh=mesh,
        in_specs=placed,
        out_specs=(P("scen", "tm", None), P("tm", "scen")),
        check_vma=False,
    )
```

```python
import functools

import jax
import jax.numpy as jnp
from jax import lax
from jax.experimental import pallas as pl
from jax.experimental.pallas import tpu as pltpu
from jax.sharding import PartitionSpec as P

SWEEPS = 2
MESH = pl.DeviceIdType.MESH
F32 = jnp.float32
BF16 = jnp.bfloat16


def kernel(
    tms, scs,
    cot_hbm, blk_hbm, links_ref, step_hbm, coup_hbm, band_ref, cand_hbm,
    out_hbm, sit_hbm,
    cot_ref, step_ref, coup_ref, cand_ref, out_ref, sit_ref, in_sem, out_sem,
    adj, sbuf, recv, tsend, trecv, wall, pick, turned, gacc, gsum, grecv,
    s_send, s_recv, t_send, t_recv, wz_send, wz_recv, wx_send, wx_recv, wy_send, wy_recv,
    wc_send, wc_recv, g_send, g_recv,
):
    me = lax.axis_index("tm")
    mine = lax.axis_index("scen")
    hours, scens, _ = cot_ref.shape
    zones, rows, bus = adj.shape
    parts, width, depth = wall.shape[:3]
    fan = links_ref.shape[1]
    share = zones // scs
    used = hours * scens
    total = tms * hours
    padded = gsum.shape[1]
    col = lax.rem(me, width)
    plane = lax.div(me, width)
    far_first = sorted(range(1, tms), key=lambda o: abs(2 * o - tms))
    both_last = (((1,), (1,)), ((), ()))

    loads = [
        pltpu.make_async_copy(src, dst, in_sem.at[i])
        for i, (src, dst) in enumerate([
            (cot_hbm, cot_ref), (step_hbm, step_ref), (blk_hbm.at[mine], wall.at[mine, col, plane]),
            (coup_hbm, coup_ref), (cand_hbm, cand_ref),
        ])
    ]
    for load in loads:
        load.start()
    barrier = pltpu.get_barrier_semaphore()
    for o in range(1, tms):
        pl.semaphore_signal(barrier, inc=1, device_id={"tm": lax.rem(me + o, tms)}, device_id_type=MESH)
    for o in range(1, scs):
        pl.semaphore_signal(barrier, inc=1, device_id={"scen": lax.rem(mine + o, scs)}, device_id_type=MESH)

    def remote(src, dst, send, got, axis, peer):
        copy = pltpu.make_async_remote_copy(
            src_ref=src, dst_ref=dst, send_sem=send, recv_sem=got,
            device_id={axis: peer}, device_id_type=MESH,
        )
        copy.start()
        return copy

    core = lax.rem(mine, 2)
    other = mine + 1 - 2 * core
    pieces = [[(0, 0)]] + [[(hop, 0), (hop, 1)] for hop in range(1, depth)]

    def held(back):
        return lax.rem(col + width - back, width)

    def on_piece(hop, way, action):
        at = plane - hop * (1 - 2 * way)
        if hop == 0:
            action(at)
        else:
            pl.when((at >= 0) & (at < depth))(lambda: action(at))

    def described(part, across, at, send, got, axis, peer):
        place = wall.at[part, across, at]
        return pltpu.make_async_remote_copy(
            src_ref=place, dst_ref=place, send_sem=send, recv_sem=got,
            device_id={axis: peer}, device_id_type=MESH,
        )

    def z_copy(hop, way, at):
        to = (plane + 1 - 2 * way) * width + col
        return described(mine, col, at, wz_send.at[way, hop], wz_recv.at[way, hop], "tm", to)

    def x_copy(o, hop, way, at, across):
        to = plane * width + lax.rem(col + o, width)
        return described(mine, across, at, wx_send.at[o, way, hop], wx_recv.at[o, way, hop], "tm", to)

    def y_copy(o, back, hop, way, at, part):
        to = lax.rem(mine + 2 * o, scs)
        return described(
            part, held(back), at, wy_send.at[o, back, way, hop], wy_recv.at[o, back, way, hop], "scen", to
        )

    def core_copy(o, back, part):
        place = wall.at[part, held(back)]
        return pltpu.make_async_remote_copy(
            src_ref=place, dst_ref=place, send_sem=wc_send.at[o, back], recv_sem=wc_recv.at[o, back],
            device_id={"scen": other}, device_id_type=MESH,
        )

    def z_sends(hop, way, at, action):
        for onward in (0, 1) if hop == 0 else (way,):
            if hop + 1 < depth:
                beyond = plane + 1 - 2 * onward
                pl.when((beyond >= 0) & (beyond < depth))(
                    lambda onward=onward: action(z_copy(hop + 1, onward, at))
                )

    def own_column(hop):
        for way in (0, 1) if hop else (0,):
            def arrived(at, way=way):
                if hop:
                    z_copy(hop, way, at).wait_recv()
                z_sends(hop, way, at, lambda copy: copy.start())
                for o in range(1, width):
                    x_copy(o, hop, way, at, col).start()
                for o in range(1, scs // 2):
                    y_copy(o, 0, hop, way, at, mine).start()

            on_piece(hop, way, arrived)

    def other_columns(hop):
        for way in (0, 1) if hop else (0,):
            def arrived(at, way=way):
                for back in range(1, width):
                    x_copy(back, hop, way, at, held(back)).wait_recv()
                    for o in range(1, scs // 2):
                        y_copy(o, back, hop, way, at, mine).start()

            on_piece(hop, way, arrived)

    def from_chips(o, back):
        for hop, way in sum(pieces, []):
            on_piece(
                hop, way,
                lambda at: y_copy(o, back, hop, way, at, lax.rem(mine + scs - 2 * o, scs)).wait_recv(),
            )

    def all_sent():
        for hop, way in sum(pieces, []):
            def gone(at):
                z_sends(hop, way, at, lambda copy: copy.wait_send())
                for o in range(1, width):
                    x_copy(o, hop, way, at, col).wait_send()
                for back in range(width):
                    for o in range(1, scs // 2):
                        y_copy(o, back, hop, way, at, mine).wait_send()

            on_piece(hop, way, gone)

    def scale(sweep, z):
        weighted = adj[z] * step_ref[z]
        sbuf[sweep, z] = weighted.astype(BF16)
        gacc[z] = weighted if sweep == 0 else gacc[z] + weighted

    def send_scaled(sweep, o):
        to = lax.rem(me + o, tms)
        return remote(
            sbuf.at[sweep, to], recv.at[sweep, me], s_send.at[sweep, o], s_recv.at[sweep, o], "tm", to
        )

    def temporal(sweep):
        side = recv[sweep].reshape(tms * rows, bus)
        copies = {}
        for o in far_first:
            to = lax.rem(me + o, tms)
            tsend[sweep, to] = jnp.dot(turned[to], side, preferred_element_type=F32).astype(BF16)
            copies[o] = remote(
                tsend.at[sweep, to], trecv.at[sweep, me], t_send.at[sweep, o], t_recv.at[sweep, o], "tm", to
            )
        trecv[sweep, me] = jnp.dot(turned[me], side, preferred_element_type=F32).astype(BF16)
        return copies

    def network(sweep):
        def one(z, _):
            picked = jnp.concatenate([sbuf[sweep, links_ref[z, k]] for k in range(fan)], axis=1)
            weights = jnp.concatenate(
                [wall[p, lax.rem(z, width), lax.div(z, width)] for p in range(parts)], axis=0
            )
            adj[z] = adj[z] - jnp.dot(picked, weights, preferred_element_type=F32)
            return 0

        lax.fori_loop(0, zones, one, 0, unroll=2)

    loads[0].wait()
    loads[1].wait()
    for z in range(zones):
        adj[z, used // 16 * 16:rows, :] = jnp.zeros((rows - used // 16 * 16, bus), F32)
        adj[z, 0:used, :] = cot_ref[:, :, z * bus:(z + 1) * bus].reshape(used, bus)
        scale(0, z)
    loads[2].wait()
    pl.semaphore_wait(barrier, tms - 1 + scs - 1)

    own_column(0)
    scaled_out = {o: send_scaled(0, o) for o in far_first}
    recv[0, me] = sbuf[0, me]

    loads[3].wait()
    loads[4].wait()
    spread = lax.broadcasted_iota(jnp.int32, (total, total), 0) - lax.broadcasted_iota(jnp.int32, (total, total), 1)
    masked = jnp.where(jnp.abs(spread) <= band_ref[0], coup_ref[...].astype(F32), 0.0).astype(BF16)
    at_row = lax.broadcasted_iota(jnp.int32, (rows, total), 0)
    ahead = at_row - scens * lax.broadcasted_iota(jnp.int32, (rows, total), 1)
    for j in range(tms):
        over = ahead + j * used
        pick[j] = jnp.where((over >= 0) & (over < scens) & (at_row < used), 1.0, 0.0).astype(BF16)

    def turn(j, _):
        half = lax.dot_general(pick[j], masked, both_last, preferred_element_type=F32).astype(BF16)
        whole = lax.dot_general(
            half, pick[...].reshape(tms * rows, total), both_last, preferred_element_type=F32
        )
        one = lax.broadcasted_iota(jnp.int32, (rows, tms * rows), 0)
        two = lax.broadcasted_iota(jnp.int32, (rows, tms * rows), 1)
        same = jnp.bitwise_and(one - two, scens - 1) == 0
        turned[j] = jnp.where(same, whole, 0.0).astype(BF16)
        return 0

    begin = 0
    for hop in range(1, depth):
        own_column(hop)
        other_columns(hop - 1)
        end = tms * hop // (depth - 1)
        lax.fori_loop(begin, end, turn, 0)
        begin = end
    other_columns(depth - 1)
    to_core = []
    for back in range(width):
        to_core.append(core_copy(0, back, mine))
        to_core[-1].start()


    for o in far_first:
        scaled_out[o].wait_recv()
    temporal_out = temporal(0)
    sent = list(scaled_out.values()) + list(temporal_out.values())

    for o in range(1, scs // 2):
        for back in range(width):
            from_chips(o, back)
            to_core.append(core_copy(o, back, lax.rem(mine + scs - 2 * o, scs)))
            to_core[-1].start()
    for copy in to_core:
        copy.wait_recv()
    sent += to_core

    network(0)
    scaled_out = {}
    for o in far_first:
        zone = lax.rem(me + o, tms)
        temporal_out[tms - o].wait_recv()
        adj[zone] = adj[zone] - trecv[0, zone].astype(F32)
        scale(1, zone)
        scaled_out[o] = send_scaled(1, o)
    adj[me] = adj[me] - trecv[0, me].astype(F32)
    scale(1, me)
    recv[1, me] = sbuf[1, me]

    network(1)

    hour_of = lax.broadcasted_iota(jnp.int32, (padded, rows), 1) - scens * lax.broadcasted_iota(
        jnp.int32, (padded, rows), 0
    )
    fold = jnp.where((hour_of >= 0) & (hour_of < scens), 1.0 / (scens * scs), 0.0)

    def fold_zone(z, _):
        gsum[z] = jnp.dot(fold, gacc[z], preferred_element_type=F32, precision=lax.Precision.HIGHEST)
        return 0

    lax.fori_loop(0, zones, fold_zone, 0)
    grads = []
    for o in range(1, scs):
        peer = lax.rem(mine + o, scs)
        grads.append(remote(
            gsum.at[pl.ds(peer * share, share)], grecv.at[o], g_send.at[o], g_recv.at[o], "scen", peer
        ))

    for o in far_first:
        scaled_out[o].wait_recv()
    temporal_out = temporal(1)
    sent += list(scaled_out.values()) + list(temporal_out.values()) + grads

    for copy in grads:
        copy.wait_recv()
    summed = gsum[pl.ds(mine * share, share)]
    for o in range(1, scs):
        summed = summed + grecv[o]
    local = cand_ref[...] - mine * (share * bus)
    siting = jnp.zeros((padded, cand_ref.shape[1]), F32)
    for part in range(share):
        ids = lax.broadcasted_iota(jnp.int32, (bus, cand_ref.shape[1]), 0) + part * bus
        chosen = jnp.where(ids == local, 1.0, 0.0)
        siting = siting + jnp.dot(
            summed[part], chosen, preferred_element_type=F32, precision=lax.Precision.HIGHEST
        )
    sit_ref[...] = siting[0:hours]
    stores = [pltpu.make_async_copy(sit_ref, sit_hbm, out_sem.at[0])]
    stores[0].start()

    def finish(zone, o):
        value = adj[zone] - trecv[1, zone].astype(F32)
        lanes = pl.ds(pl.multiple_of(zone * bus, bus), bus)
        out_ref[:, :, lanes] = value[0:used].reshape(hours, scens, bus)
        store = pltpu.make_async_copy(out_ref.at[:, :, lanes], out_hbm.at[:, :, lanes], out_sem.at[o + 1])
        store.start()
        stores.append(store)

    finish(me, 0)
    for o in far_first:
        temporal_out[tms - o].wait_recv()
        finish(lax.rem(me + o, tms), o)
    for copy in sent:
        copy.wait_send()
    all_sent()
    for store in stores:
        store.wait()


def hand_on(adj_in, sit_in, adj_out, sit_out, sem):
    hours = adj_in.shape[0]
    cuts = 7 if hours % 7 == 0 else 1
    step = hours // cuts
    copies = [pltpu.make_async_copy(sit_in, sit_out, sem.at[cuts])]
    for i in range(cuts):
        rows = pl.ds(i * step, step)
        copies.append(pltpu.make_async_copy(adj_in.at[rows], adj_out.at[rows], sem.at[i]))
    for copy in copies:
        copy.start()
    for copy in copies:
        copy.wait()


def per_device(tms, scs, cotangent, blocks, zone_links, step_size, coupling, ramp_band, candidates):
    scens, hours, buses = cotangent.shape
    _, fan, bus, _ = blocks.shape
    zones = buses // bus
    rows = -(-hours * scens // 16) * 16
    padded = -(-hours // 8) * 8
    cut = fan * bus // scs
    width = 1
    while 4 * width * width <= tms:
        width *= 2
    depth = tms // width
    hbm = pl.BlockSpec(memory_space=pltpu.HBM)
    smem = pl.BlockSpec(memory_space=pltpu.SMEM)
    dma = pltpu.SemaphoreType.DMA
    adjoint, siting_gradient = pl.pallas_call(
        functools.partial(kernel, tms, scs),
        out_shape=(
            jax.ShapeDtypeStruct((hours, scens, buses), F32),
            jax.ShapeDtypeStruct((hours, candidates.shape[0]), F32),
        ),
        in_specs=[hbm, hbm, smem, hbm, hbm, smem, hbm],
        out_specs=(hbm, hbm),
        scratch_shapes=[
            pltpu.VMEM((hours, scens, buses), F32),
            pltpu.VMEM((zones, 1, bus), F32),
            pltpu.VMEM(coupling.shape[1:], BF16),
            pltpu.VMEM((1, candidates.shape[0]), jnp.int32),
            pltpu.VMEM((hours, scens, buses), F32),
            pltpu.VMEM((hours, candidates.shape[0]), F32),
            dma((5,)), dma((tms + 1,)),
            pltpu.VMEM((zones, rows, bus), F32),
            pltpu.VMEM((SWEEPS, zones, rows, bus), BF16),
            pltpu.VMEM((SWEEPS, tms, rows, bus), BF16),
            pltpu.VMEM((SWEEPS, tms, rows, bus), BF16),
            pltpu.VMEM((SWEEPS, zones, rows, bus), BF16),
            pltpu.VMEM((scs, width, depth, cut, bus), BF16),
            pltpu.VMEM((tms, rows, tms * hours), BF16),
            pltpu.VMEM((tms, rows, tms * rows), BF16),
            pltpu.VMEM((zones, rows, bus), F32),
            pltpu.VMEM((zones, padded, bus), F32),
            pltpu.VMEM((scs, zones // scs, padded, bus), F32),
            dma((SWEEPS, tms)), dma((SWEEPS, tms)), dma((SWEEPS, tms)), dma((SWEEPS, tms)),
            dma((2, depth)), dma((2, depth)), dma((width, 2, depth)), dma((width, 2, depth)),
            dma((scs, width, 2, depth)), dma((scs, width, 2, depth)), dma((scs, width)), dma((scs, width)),
            dma((scs,)), dma((scs,)),
        ],
        compiler_params=pltpu.CompilerParams(
            collective_id=0, has_side_effects=True, vmem_limit_bytes=62 * 1024 * 1024
        ),
        name="sweeps",
    )(
        jnp.transpose(cotangent, (1, 0, 2)),
        blocks.reshape(scs, cut, bus),
        zone_links,
        step_size.reshape(zones, 1, bus),
        coupling.reshape(coupling.shape[1:]),
        ramp_band,
        candidates.reshape(1, -1),
    )
    adjoint, siting_gradient = pl.pallas_call(
        hand_on,
        out_shape=(
            jax.ShapeDtypeStruct(adjoint.shape, F32),
            jax.ShapeDtypeStruct(siting_gradient.shape, F32),
        ),
        in_specs=[hbm, hbm],
        out_specs=(hbm, hbm),
        scratch_shapes=[dma((8,))],
        compiler_params=pltpu.CompilerParams(vmem_limit_bytes=62 * 1024 * 1024),
        name="hand_on",
    )(adjoint, siting_gradient)
    return jnp.transpose(adjoint, (1, 0, 2)), siting_gradient


def solution(mesh):
    placed = (
        P("scen", "tm", None),
        P("tm", None, None, None),
        P(),
        P(),
        P("tm", None, None),
        P("tm"),
        P("scen"),
    )
    return jax.shard_map(
        functools.partial(per_device, mesh.shape["tm"], mesh.shape["scen"]),
        mesh=mesh,
        in_specs=placed,
        out_specs=(P("scen", "tm", None), P("tm", "scen")),
        check_vma=False,
    )
```

```python
import functools

import jax
import jax.numpy as jnp
from jax import lax
from jax.experimental import pallas as pl
from jax.experimental.pallas import tpu as pltpu
from jax.sharding import PartitionSpec as P

SWEEPS = 2
MESH = pl.DeviceIdType.MESH
F32 = jnp.float32
BF16 = jnp.bfloat16


def kernel(
    tms, scs,
    cot_hbm, blk_hbm, links_ref, step_hbm, coup_hbm, band_ref, cand_hbm,
    out_hbm, sit_hbm,
    cot_ref, step_ref, coup_ref, cand_ref, out_ref, sit_ref, in_sem, out_sem,
    adj, sbuf, recv, tsend, trecv, wall, turned, spread_in, spread_out, gacc, gsum, grecv,
    s_send, s_recv, t_send, t_recv, wz_send, wz_recv, wx_send, wx_recv, wy_send, wy_recv,
    wc_send, wc_recv, g_send, g_recv,
):
    me = lax.axis_index("tm")
    mine = lax.axis_index("scen")
    hours, scens, _ = cot_ref.shape
    zones, rows, bus = adj.shape
    parts, width, depth = wall.shape[:3]
    fan = links_ref.shape[1]
    share = zones // scs
    used = hours * scens
    total = tms * hours
    padded = gsum.shape[1]
    slot = rows // scens
    col = lax.rem(me, width)
    plane = lax.div(me, width)
    far_first = sorted(range(1, tms), key=lambda o: abs(2 * o - tms))
    both_last = (((1,), (1,)), ((), ()))

    loads = [
        pltpu.make_async_copy(src, dst, in_sem.at[i])
        for i, (src, dst) in enumerate([
            (cot_hbm, cot_ref), (step_hbm, step_ref), (blk_hbm.at[mine], wall.at[mine, col, plane]),
            (coup_hbm, coup_ref), (cand_hbm, cand_ref),
        ])
    ]
    for load in loads:
        load.start()
    barrier = pltpu.get_barrier_semaphore()
    for o in range(1, tms):
        pl.semaphore_signal(barrier, inc=1, device_id={"tm": lax.rem(me + o, tms)}, device_id_type=MESH)
    for o in range(1, scs):
        pl.semaphore_signal(barrier, inc=1, device_id={"scen": lax.rem(mine + o, scs)}, device_id_type=MESH)

    def remote(src, dst, send, got, axis, peer):
        copy = pltpu.make_async_remote_copy(
            src_ref=src, dst_ref=dst, send_sem=send, recv_sem=got,
            device_id={axis: peer}, device_id_type=MESH,
        )
        copy.start()
        return copy

    def scale(sweep, z):
        weighted = adj[z] * step_ref[z]
        sbuf[sweep, z] = weighted.astype(BF16)
        gacc[z] = weighted if sweep == 0 else gacc[z] + weighted

    def send_scaled(sweep, o):
        to = lax.rem(me + o, tms)
        return remote(
            sbuf.at[sweep, to], recv.at[sweep, me], s_send.at[sweep, o], s_recv.at[sweep, o], "tm", to
        )

    def temporal(sweep):
        spread_in[...] = recv[sweep].reshape(tms * rows, bus).astype(F32)
        side = jnp.concatenate(
            [spread_in[pl.ds(s, tms * slot, stride=scens), :].astype(BF16) for s in range(scens)], axis=1
        )
        term = jnp.dot(turned[...], side, preferred_element_type=F32)
        for s in range(scens):
            spread_out[pl.ds(s, tms * slot, stride=scens), :] = term[:, s * bus:(s + 1) * bus]
        tsend[sweep] = spread_out[...].reshape(tms, rows, bus).astype(BF16)
        copies = {}
        for o in far_first:
            to = lax.rem(me + o, tms)
            copies[o] = remote(
                tsend.at[sweep, to], trecv.at[sweep, me], t_send.at[sweep, o], t_recv.at[sweep, o], "tm", to
            )
        trecv[sweep, me] = tsend[sweep, me]
        return copies

    def network(sweep):
        def one(z, _):
            picked = jnp.concatenate([sbuf[sweep, links_ref[z, k]] for k in range(fan)], axis=1)
            weights = jnp.concatenate(
                [wall[p, lax.rem(z, width), lax.div(z, width)] for p in range(parts)], axis=0
            )
            adj[z] = adj[z] - jnp.dot(picked, weights, preferred_element_type=F32)
            return 0

        lax.fori_loop(0, zones, one, 0, unroll=2)

    loads[0].wait()
    loads[1].wait()
    for z in range(zones):
        adj[z, used // 16 * 16:rows, :] = jnp.zeros((rows - used // 16 * 16, bus), F32)
        adj[z, 0:used, :] = cot_ref[:, :, z * bus:(z + 1) * bus].reshape(used, bus)
        scale(0, z)
    loads[2].wait()
    pl.semaphore_wait(barrier, tms - 1 + scs - 1)

    along_z = []
    for o in range(1, depth):
        to = lax.rem(plane + o, depth) * width + col
        piece = wall.at[mine, col, plane]
        along_z.append(remote(piece, piece, wz_send.at[o], wz_recv.at[o], "tm", to))
    scaled_out = {o: send_scaled(0, o) for o in far_first}
    recv[0, me] = sbuf[0, me]

    loads[3].wait()
    loads[4].wait()
    spread = lax.broadcasted_iota(jnp.int32, (total, total), 0) - lax.broadcasted_iota(jnp.int32, (total, total), 1)
    masked = jnp.where(jnp.abs(spread) <= band_ref[0], coup_ref[...].astype(F32), 0.0).astype(BF16)
    wide = lax.broadcasted_iota(jnp.int32, (tms * slot, 1), 0)
    device = jnp.zeros_like(wide)
    for j in range(1, tms):
        device = device + (wide >= j * slot).astype(jnp.int32)
    within = wide - device * slot
    hour = jnp.where(within < hours, device * hours + within, -1)
    pick = jnp.where(hour == lax.broadcasted_iota(jnp.int32, (tms * slot, total), 1), 1.0, 0.0).astype(BF16)
    half = lax.dot_general(pick, masked, both_last, preferred_element_type=F32).astype(BF16)
    turned[...] = lax.dot_general(half, pick, both_last, preferred_element_type=F32).astype(BF16)

    core = lax.rem(mine, 2)
    along_y = {}

    def to_same_core(back):
        held = lax.rem(col + width - back, width)
        for o in range(1, scs // 2):
            piece = wall.at[mine, held]
            along_y[o, back] = remote(
                piece, piece, wy_send.at[o, back], wy_recv.at[o, back], "scen", lax.rem(mine + 2 * o, scs)
            )

    for copy in along_z:
        copy.wait_recv()
    along_x = []
    for o in range(1, width):
        piece = wall.at[mine, col]
        to = plane * width + lax.rem(col + o, width)
        along_x.append(remote(piece, piece, wx_send.at[o], wx_recv.at[o], "tm", to))
    to_same_core(0)
    for o in range(1, width):
        along_x[o - 1].wait_recv()
        to_same_core(o)

    for o in far_first:
        scaled_out[o].wait_recv()
    temporal_out = temporal(0)
    sent = along_z + along_x + list(along_y.values()) + list(scaled_out.values()) + list(temporal_out.values())

    to_core = []
    for o in range(scs // 2):
        if o > 0:
            for back in range(width):
                along_y[o, back].wait_recv()
        piece = wall.at[lax.rem(mine + scs - 2 * o, scs)]
        to_core.append(remote(piece, piece, wc_send.at[o], wc_recv.at[o], "scen", mine + 1 - 2 * core))
    for copy in to_core:
        copy.wait_recv()
    sent += to_core

    network(0)
    scaled_out = {}
    for o in far_first:
        zone = lax.rem(me + o, tms)
        temporal_out[tms - o].wait_recv()
        adj[zone] = adj[zone] - trecv[0, zone].astype(F32)
        scale(1, zone)
        scaled_out[o] = send_scaled(1, o)
    adj[me] = adj[me] - trecv[0, me].astype(F32)
    scale(1, me)
    recv[1, me] = sbuf[1, me]

    network(1)

    hour_of = lax.broadcasted_iota(jnp.int32, (padded, rows), 1) - scens * lax.broadcasted_iota(
        jnp.int32, (padded, rows), 0
    )
    fold = jnp.where((hour_of >= 0) & (hour_of < scens), 1.0 / (scens * scs), 0.0)

    def fold_zone(z, _):
        gsum[z] = jnp.dot(fold, gacc[z], preferred_element_type=F32, precision=lax.Precision.HIGHEST)
        return 0

    lax.fori_loop(0, zones, fold_zone, 0)
    grads = []
    for o in range(1, scs):
        peer = lax.rem(mine + o, scs)
        grads.append(remote(
            gsum.at[pl.ds(peer * share, share)], grecv.at[o], g_send.at[o], g_recv.at[o], "scen", peer
        ))

    for o in far_first:
        scaled_out[o].wait_recv()
    temporal_out = temporal(1)
    sent += list(scaled_out.values()) + list(temporal_out.values()) + grads

    for copy in grads:
        copy.wait_recv()
    summed = gsum[pl.ds(mine * share, share)]
    for o in range(1, scs):
        summed = summed + grecv[o]
    local = cand_ref[...] - mine * (share * bus)
    siting = jnp.zeros((padded, cand_ref.shape[1]), F32)
    for part in range(share):
        ids = lax.broadcasted_iota(jnp.int32, (bus, cand_ref.shape[1]), 0) + part * bus
        chosen = jnp.where(ids == local, 1.0, 0.0)
        siting = siting + jnp.dot(
            summed[part], chosen, preferred_element_type=F32, precision=lax.Precision.HIGHEST
        )
    sit_ref[...] = siting[0:hours]
    stores = [pltpu.make_async_copy(sit_ref, sit_hbm, out_sem.at[0])]
    stores[0].start()

    def finish(zone, o):
        value = adj[zone] - trecv[1, zone].astype(F32)
        lanes = pl.ds(pl.multiple_of(zone * bus, bus), bus)
        out_ref[:, :, lanes] = value[0:used].reshape(hours, scens, bus)
        store = pltpu.make_async_copy(out_ref.at[:, :, lanes], out_hbm.at[:, :, lanes], out_sem.at[o + 1])
        store.start()
        stores.append(store)

    finish(me, 0)
    for o in far_first:
        temporal_out[tms - o].wait_recv()
        finish(lax.rem(me + o, tms), o)
    for copy in sent:
        copy.wait_send()
    for store in stores:
        store.wait()


def hand_on(adj_in, sit_in, adj_out, sit_out, adj, sit, sem):
    hours = adj_in.shape[0]
    cuts = 3 if hours % 3 == 0 else 1
    step = hours // cuts
    spans = [pl.ds(i * step, step) for i in range(cuts)]
    legs = [(sit_in, sit, sit_out)] + [(adj_in.at[at], adj.at[at], adj_out.at[at]) for at in spans]
    inward = [pltpu.make_async_copy(src, mid, sem.at[0, i]) for i, (src, mid, _) in enumerate(legs)]
    outward = [pltpu.make_async_copy(mid, dst, sem.at[1, i]) for i, (_, mid, dst) in enumerate(legs)]
    for copy in inward:
        copy.start()
    for first, second in zip(inward, outward):
        first.wait()
        second.start()
    for copy in outward:
        copy.wait()


def per_device(tms, scs, cotangent, blocks, zone_links, step_size, coupling, ramp_band, candidates):
    scens, hours, buses = cotangent.shape
    _, fan, bus, _ = blocks.shape
    zones = buses // bus
    rows = -(-hours * scens // 16) * 16
    padded = -(-hours // 8) * 8
    cut = fan * bus // scs
    width = 1
    while 4 * width * width <= tms:
        width *= 2
    depth = tms // width
    hbm = pl.BlockSpec(memory_space=pltpu.HBM)
    smem = pl.BlockSpec(memory_space=pltpu.SMEM)
    dma = pltpu.SemaphoreType.DMA
    adjoint, siting_gradient = pl.pallas_call(
        functools.partial(kernel, tms, scs),
        out_shape=(
            jax.ShapeDtypeStruct((hours, scens, buses), F32),
            jax.ShapeDtypeStruct((hours, candidates.shape[0]), F32),
        ),
        in_specs=[hbm, hbm, smem, hbm, hbm, smem, hbm],
        out_specs=(hbm, hbm),
        scratch_shapes=[
            pltpu.VMEM((hours, scens, buses), F32),
            pltpu.VMEM((zones, 1, bus), F32),
            pltpu.VMEM(coupling.shape[1:], BF16),
            pltpu.VMEM((1, candidates.shape[0]), jnp.int32),
            pltpu.VMEM((hours, scens, buses), F32),
            pltpu.VMEM((hours, candidates.shape[0]), F32),
            dma((5,)), dma((tms + 1,)),
            pltpu.VMEM((zones, rows, bus), F32),
            pltpu.VMEM((SWEEPS, zones, rows, bus), BF16),
            pltpu.VMEM((SWEEPS, tms, rows, bus), BF16),
            pltpu.VMEM((SWEEPS, tms, rows, bus), BF16),
            pltpu.VMEM((SWEEPS, zones, rows, bus), BF16),
            pltpu.VMEM((scs, width, depth, cut, bus), BF16),
            pltpu.VMEM((tms * (rows // scens), tms * (rows // scens)), BF16),
            pltpu.VMEM((tms * rows, bus), F32),
            pltpu.VMEM((tms * rows, bus), F32),
            pltpu.VMEM((zones, rows, bus), F32),
            pltpu.VMEM((zones, padded, bus), F32),
            pltpu.VMEM((scs, zones // scs, padded, bus), F32),
            dma((SWEEPS, tms)), dma((SWEEPS, tms)), dma((SWEEPS, tms)), dma((SWEEPS, tms)),
            dma((depth,)), dma((depth,)), dma((width,)), dma((width,)),
            dma((scs, width)), dma((scs, width)), dma((scs,)), dma((scs,)), dma((scs,)), dma((scs,)),
        ],
        compiler_params=pltpu.CompilerParams(
            collective_id=0, has_side_effects=True, vmem_limit_bytes=62 * 1024 * 1024
        ),
        name="sweeps",
    )(
        jnp.transpose(cotangent, (1, 0, 2)),
        blocks.reshape(scs, cut, bus),
        zone_links,
        step_size.reshape(zones, 1, bus),
        coupling.reshape(coupling.shape[1:]),
        ramp_band,
        candidates.reshape(1, -1),
    )
    adjoint, siting_gradient = pl.pallas_call(
        hand_on,
        out_shape=(
            jax.ShapeDtypeStruct(adjoint.shape, F32),
            jax.ShapeDtypeStruct(siting_gradient.shape, F32),
        ),
        in_specs=[hbm, hbm],
        out_specs=(hbm, hbm),
        scratch_shapes=[
            pltpu.VMEM(adjoint.shape, F32), pltpu.VMEM(siting_gradient.shape, F32), dma((2, 4)),
        ],
        compiler_params=pltpu.CompilerParams(vmem_limit_bytes=62 * 1024 * 1024),
        name="hand_on",
    )(adjoint, siting_gradient)
    return jnp.transpose(adjoint, (1, 0, 2)), siting_gradient


def solution(mesh):
    placed = (
        P("scen", "tm", None),
        P("tm", None, None, None),
        P(),
        P(),
        P("tm", None, None),
        P("tm"),
        P("scen"),
    )
    return jax.shard_map(
        functools.partial(per_device, mesh.shape["tm"], mesh.shape["scen"]),
        mesh=mesh,
        in_specs=placed,
        out_specs=(P("scen", "tm", None), P("tm", "scen")),
        check_vma=False,
    )
```

```python
import functools

import jax
import jax.numpy as jnp
from jax import lax
from jax.experimental import pallas as pl
from jax.experimental.pallas import tpu as pltpu
from jax.sharding import PartitionSpec as P

SWEEPS = 2
MESH = pl.DeviceIdType.MESH
F32 = jnp.float32
BF16 = jnp.bfloat16


def kernel(
    tms, scs,
    cot_hbm, blk_hbm, links_ref, step_hbm, coup_hbm, band_ref, cand_hbm,
    out_hbm, sit_hbm,
    cot_ref, step_ref, coup_ref, cand_ref, out_ref, sit_ref, in_sem, out_sem,
    adj, sbuf, recv, tsend, trecv, wall, turned, spread_in, spread_out, gacc, gsum, grecv,
    s_send, s_recv, t_send, t_recv, wz_send, wz_recv, wx_send, wx_recv, wy_send, wy_recv,
    wc_send, wc_recv, g_send, g_recv,
):
    me = lax.axis_index("tm")
    mine = lax.axis_index("scen")
    hours, scens, _ = cot_ref.shape
    zones, rows, bus = adj.shape
    parts, width, depth = wall.shape[:3]
    fan = links_ref.shape[1]
    share = zones // scs
    used = hours * scens
    total = tms * hours
    padded = gsum.shape[1]
    slot = rows // scens
    col = lax.rem(me, width)
    plane = lax.div(me, width)
    far_first = sorted(range(1, tms), key=lambda o: abs(2 * o - tms))
    both_last = (((1,), (1,)), ((), ()))

    loads = [
        pltpu.make_async_copy(src, dst, in_sem.at[i])
        for i, (src, dst) in enumerate([
            (cot_hbm, cot_ref), (step_hbm, step_ref), (blk_hbm.at[mine], wall.at[mine, col, plane]),
            (coup_hbm, coup_ref), (cand_hbm, cand_ref),
        ])
    ]
    for load in loads:
        load.start()
    barrier = pltpu.get_barrier_semaphore()
    for o in range(1, tms):
        pl.semaphore_signal(barrier, inc=1, device_id={"tm": lax.rem(me + o, tms)}, device_id_type=MESH)
    for o in range(1, scs):
        pl.semaphore_signal(barrier, inc=1, device_id={"scen": lax.rem(mine + o, scs)}, device_id_type=MESH)

    def remote(src, dst, send, got, axis, peer):
        copy = pltpu.make_async_remote_copy(
            src_ref=src, dst_ref=dst, send_sem=send, recv_sem=got,
            device_id={axis: peer}, device_id_type=MESH,
        )
        copy.start()
        return copy

    core = lax.rem(mine, 2)
    other = mine + 1 - 2 * core
    pieces = [[(0, 0)]] + [[(hop, 0), (hop, 1)] for hop in range(1, depth)]

    def held(back):
        return lax.rem(col + width - back, width)

    def on_piece(hop, way, action):
        at = plane - hop * (1 - 2 * way)
        if hop == 0:
            action(at)
        else:
            pl.when((at >= 0) & (at < depth))(lambda: action(at))

    def described(part, across, at, send, got, axis, peer):
        place = wall.at[part, across, at]
        return pltpu.make_async_remote_copy(
            src_ref=place, dst_ref=place, send_sem=send, recv_sem=got,
            device_id={axis: peer}, device_id_type=MESH,
        )

    def z_copy(hop, way, at):
        to = (plane + 1 - 2 * way) * width + col
        return described(mine, col, at, wz_send.at[way, hop], wz_recv.at[way, hop], "tm", to)

    def x_copy(o, hop, way, at, across):
        to = plane * width + lax.rem(col + o, width)
        return described(mine, across, at, wx_send.at[o, way, hop], wx_recv.at[o, way, hop], "tm", to)

    def y_copy(o, back, hop, way, at, part):
        to = lax.rem(mine + 2 * o, scs)
        return described(
            part, held(back), at, wy_send.at[o, back, way, hop], wy_recv.at[o, back, way, hop], "scen", to
        )

    def core_copy(o, back, part):
        place = wall.at[part, held(back)]
        return pltpu.make_async_remote_copy(
            src_ref=place, dst_ref=place, send_sem=wc_send.at[o, back], recv_sem=wc_recv.at[o, back],
            device_id={"scen": other}, device_id_type=MESH,
        )

    def z_sends(hop, way, at, action):
        for onward in (0, 1) if hop == 0 else (way,):
            if hop + 1 < depth:
                beyond = plane + 1 - 2 * onward
                pl.when((beyond >= 0) & (beyond < depth))(
                    lambda onward=onward: action(z_copy(hop + 1, onward, at))
                )

    def own_column(hop):
        for way in (0, 1) if hop else (0,):
            def arrived(at, way=way):
                if hop:
                    z_copy(hop, way, at).wait_recv()
                z_sends(hop, way, at, lambda copy: copy.start())
                for o in range(1, width):
                    x_copy(o, hop, way, at, col).start()
                for o in range(1, scs // 2):
                    y_copy(o, 0, hop, way, at, mine).start()

            on_piece(hop, way, arrived)

    def other_columns(hop):
        for way in (0, 1) if hop else (0,):
            def arrived(at, way=way):
                for back in range(1, width):
                    x_copy(back, hop, way, at, held(back)).wait_recv()
                    for o in range(1, scs // 2):
                        y_copy(o, back, hop, way, at, mine).start()

            on_piece(hop, way, arrived)

    def from_chips(o, back):
        for hop, way in sum(pieces, []):
            on_piece(
                hop, way,
                lambda at: y_copy(o, back, hop, way, at, lax.rem(mine + scs - 2 * o, scs)).wait_recv(),
            )

    def all_sent():
        for hop, way in sum(pieces, []):
            def gone(at):
                z_sends(hop, way, at, lambda copy: copy.wait_send())
                for o in range(1, width):
                    x_copy(o, hop, way, at, col).wait_send()
                for back in range(width):
                    for o in range(1, scs // 2):
                        y_copy(o, back, hop, way, at, mine).wait_send()

            on_piece(hop, way, gone)

    def scale(sweep, z):
        weighted = adj[z] * step_ref[z]
        sbuf[sweep, z] = weighted.astype(BF16)
        gacc[z] = weighted if sweep == 0 else gacc[z] + weighted

    def send_scaled(sweep, o):
        to = lax.rem(me + o, tms)
        return remote(
            sbuf.at[sweep, to], recv.at[sweep, me], s_send.at[sweep, o], s_recv.at[sweep, o], "tm", to
        )

    def temporal(sweep):
        spread_in[...] = recv[sweep].reshape(tms * rows, bus).astype(F32)
        side = jnp.concatenate(
            [spread_in[pl.ds(s, tms * slot, stride=scens), :].astype(BF16) for s in range(scens)], axis=1
        )
        term = jnp.dot(turned[...], side, preferred_element_type=F32)
        for s in range(scens):
            spread_out[pl.ds(s, tms * slot, stride=scens), :] = term[:, s * bus:(s + 1) * bus]
        tsend[sweep] = spread_out[...].reshape(tms, rows, bus).astype(BF16)
        copies = {}
        for o in far_first:
            to = lax.rem(me + o, tms)
            copies[o] = remote(
                tsend.at[sweep, to], trecv.at[sweep, me], t_send.at[sweep, o], t_recv.at[sweep, o], "tm", to
            )
        trecv[sweep, me] = tsend[sweep, me]
        return copies

    def network(sweep):
        def one(z, _):
            picked = jnp.concatenate([sbuf[sweep, links_ref[z, k]] for k in range(fan)], axis=1)
            weights = jnp.concatenate(
                [wall[p, lax.rem(z, width), lax.div(z, width)] for p in range(parts)], axis=0
            )
            adj[z] = adj[z] - jnp.dot(picked, weights, preferred_element_type=F32)
            return 0

        lax.fori_loop(0, zones, one, 0, unroll=2)

    loads[0].wait()
    loads[1].wait()
    for z in range(zones):
        adj[z, used // 16 * 16:rows, :] = jnp.zeros((rows - used // 16 * 16, bus), F32)
        adj[z, 0:used, :] = cot_ref[:, :, z * bus:(z + 1) * bus].reshape(used, bus)
        scale(0, z)
    loads[2].wait()
    pl.semaphore_wait(barrier, tms - 1 + scs - 1)

    own_column(0)
    scaled_out = {o: send_scaled(0, o) for o in far_first}
    recv[0, me] = sbuf[0, me]

    loads[3].wait()
    loads[4].wait()
    spread = lax.broadcasted_iota(jnp.int32, (total, total), 0) - lax.broadcasted_iota(jnp.int32, (total, total), 1)
    masked = jnp.where(jnp.abs(spread) <= band_ref[0], coup_ref[...].astype(F32), 0.0).astype(BF16)
    wide = lax.broadcasted_iota(jnp.int32, (tms * slot, 1), 0)
    device = jnp.zeros_like(wide)
    for j in range(1, tms):
        device = device + (wide >= j * slot).astype(jnp.int32)
    within = wide - device * slot
    hour = jnp.where(within < hours, device * hours + within, -1)
    pick = jnp.where(hour == lax.broadcasted_iota(jnp.int32, (tms * slot, total), 1), 1.0, 0.0).astype(BF16)
    half = lax.dot_general(pick, masked, both_last, preferred_element_type=F32).astype(BF16)
    turned[...] = lax.dot_general(half, pick, both_last, preferred_element_type=F32).astype(BF16)

    for hop in range(1, depth):
        own_column(hop)
        other_columns(hop - 1)
    other_columns(depth - 1)
    to_core = []
    for back in range(width):
        to_core.append(core_copy(0, back, mine))
        to_core[-1].start()

    for o in far_first:
        scaled_out[o].wait_recv()
    temporal_out = temporal(0)
    sent = list(scaled_out.values()) + list(temporal_out.values())

    for o in range(1, scs // 2):
        for back in range(width):
            from_chips(o, back)
            to_core.append(core_copy(o, back, lax.rem(mine + scs - 2 * o, scs)))
            to_core[-1].start()
    for copy in to_core:
        copy.wait_recv()
    sent += to_core

    network(0)
    scaled_out = {}
    for o in far_first:
        zone = lax.rem(me + o, tms)
        temporal_out[tms - o].wait_recv()
        adj[zone] = adj[zone] - trecv[0, zone].astype(F32)
        scale(1, zone)
        scaled_out[o] = send_scaled(1, o)
    adj[me] = adj[me] - trecv[0, me].astype(F32)
    scale(1, me)
    recv[1, me] = sbuf[1, me]

    network(1)

    hour_of = lax.broadcasted_iota(jnp.int32, (padded, rows), 1) - scens * lax.broadcasted_iota(
        jnp.int32, (padded, rows), 0
    )
    fold = jnp.where((hour_of >= 0) & (hour_of < scens), 1.0 / (scens * scs), 0.0)

    def fold_zone(z, _):
        gsum[z] = jnp.dot(fold, gacc[z], preferred_element_type=F32, precision=lax.Precision.HIGHEST)
        return 0

    lax.fori_loop(0, zones, fold_zone, 0)
    grads = []
    for o in range(1, scs):
        peer = lax.rem(mine + o, scs)
        grads.append(remote(
            gsum.at[pl.ds(peer * share, share)], grecv.at[o], g_send.at[o], g_recv.at[o], "scen", peer
        ))

    for o in far_first:
        scaled_out[o].wait_recv()
    temporal_out = temporal(1)
    sent += list(scaled_out.values()) + list(temporal_out.values()) + grads

    for copy in grads:
        copy.wait_recv()
    summed = gsum[pl.ds(mine * share, share)]
    for o in range(1, scs):
        summed = summed + grecv[o]
    local = cand_ref[...] - mine * (share * bus)
    siting = jnp.zeros((padded, cand_ref.shape[1]), F32)
    for part in range(share):
        ids = lax.broadcasted_iota(jnp.int32, (bus, cand_ref.shape[1]), 0) + part * bus
        chosen = jnp.where(ids == local, 1.0, 0.0)
        siting = siting + jnp.dot(
            summed[part], chosen, preferred_element_type=F32, precision=lax.Precision.HIGHEST
        )
    sit_ref[...] = siting[0:hours]
    stores = [pltpu.make_async_copy(sit_ref, sit_hbm, out_sem.at[0])]
    stores[0].start()

    def finish(zone, o):
        value = adj[zone] - trecv[1, zone].astype(F32)
        lanes = pl.ds(pl.multiple_of(zone * bus, bus), bus)
        out_ref[:, :, lanes] = value[0:used].reshape(hours, scens, bus)
        store = pltpu.make_async_copy(out_ref.at[:, :, lanes], out_hbm.at[:, :, lanes], out_sem.at[o + 1])
        store.start()
        stores.append(store)

    finish(me, 0)
    for o in far_first:
        temporal_out[tms - o].wait_recv()
        finish(lax.rem(me + o, tms), o)
    for copy in sent:
        copy.wait_send()
    all_sent()
    for store in stores:
        store.wait()


def hand_on(adj_in, sit_in, adj_out, sit_out, adj, sit, sem):
    hours = adj_in.shape[0]
    cuts = 3 if hours % 3 == 0 else 1
    step = hours // cuts
    spans = [pl.ds(i * step, step) for i in range(cuts)]
    legs = [(sit_in, sit, sit_out)] + [(adj_in.at[at], adj.at[at], adj_out.at[at]) for at in spans]
    inward = [pltpu.make_async_copy(src, mid, sem.at[0, i]) for i, (src, mid, _) in enumerate(legs)]
    outward = [pltpu.make_async_copy(mid, dst, sem.at[1, i]) for i, (_, mid, dst) in enumerate(legs)]
    for copy in inward:
        copy.start()
    for first, second in zip(inward, outward):
        first.wait()
        second.start()
    for copy in outward:
        copy.wait()


def per_device(tms, scs, cotangent, blocks, zone_links, step_size, coupling, ramp_band, candidates):
    scens, hours, buses = cotangent.shape
    _, fan, bus, _ = blocks.shape
    zones = buses // bus
    rows = -(-hours * scens // 16) * 16
    padded = -(-hours // 8) * 8
    cut = fan * bus // scs
    width = 1
    while 4 * width * width <= tms:
        width *= 2
    depth = tms // width
    hbm = pl.BlockSpec(memory_space=pltpu.HBM)
    smem = pl.BlockSpec(memory_space=pltpu.SMEM)
    dma = pltpu.SemaphoreType.DMA
    adjoint, siting_gradient = pl.pallas_call(
        functools.partial(kernel, tms, scs),
        out_shape=(
            jax.ShapeDtypeStruct((hours, scens, buses), F32),
            jax.ShapeDtypeStruct((hours, candidates.shape[0]), F32),
        ),
        in_specs=[hbm, hbm, smem, hbm, hbm, smem, hbm],
        out_specs=(hbm, hbm),
        scratch_shapes=[
            pltpu.VMEM((hours, scens, buses), F32),
            pltpu.VMEM((zones, 1, bus), F32),
            pltpu.VMEM(coupling.shape[1:], BF16),
            pltpu.VMEM((1, candidates.shape[0]), jnp.int32),
            pltpu.VMEM((hours, scens, buses), F32),
            pltpu.VMEM((hours, candidates.shape[0]), F32),
            dma((5,)), dma((tms + 1,)),
            pltpu.VMEM((zones, rows, bus), F32),
            pltpu.VMEM((SWEEPS, zones, rows, bus), BF16),
            pltpu.VMEM((SWEEPS, tms, rows, bus), BF16),
            pltpu.VMEM((SWEEPS, tms, rows, bus), BF16),
            pltpu.VMEM((SWEEPS, zones, rows, bus), BF16),
            pltpu.VMEM((scs, width, depth, cut, bus), BF16),
            pltpu.VMEM((tms * (rows // scens), tms * (rows // scens)), BF16),
            pltpu.VMEM((tms * rows, bus), F32),
            pltpu.VMEM((tms * rows, bus), F32),
            pltpu.VMEM((zones, rows, bus), F32),
            pltpu.VMEM((zones, padded, bus), F32),
            pltpu.VMEM((scs, zones // scs, padded, bus), F32),
            dma((SWEEPS, tms)), dma((SWEEPS, tms)), dma((SWEEPS, tms)), dma((SWEEPS, tms)),
            dma((2, depth)), dma((2, depth)), dma((width, 2, depth)), dma((width, 2, depth)),
            dma((scs, width, 2, depth)), dma((scs, width, 2, depth)), dma((scs, width)), dma((scs, width)),
            dma((scs,)), dma((scs,)),
        ],
        compiler_params=pltpu.CompilerParams(
            collective_id=0, has_side_effects=True, vmem_limit_bytes=62 * 1024 * 1024
        ),
        name="sweeps",
    )(
        jnp.transpose(cotangent, (1, 0, 2)),
        blocks.reshape(scs, cut, bus),
        zone_links,
        step_size.reshape(zones, 1, bus),
        coupling.reshape(coupling.shape[1:]),
        ramp_band,
        candidates.reshape(1, -1),
    )
    adjoint, siting_gradient = pl.pallas_call(
        hand_on,
        out_shape=(
            jax.ShapeDtypeStruct(adjoint.shape, F32),
            jax.ShapeDtypeStruct(siting_gradient.shape, F32),
        ),
        in_specs=[hbm, hbm],
        out_specs=(hbm, hbm),
        scratch_shapes=[
            pltpu.VMEM(adjoint.shape, F32), pltpu.VMEM(siting_gradient.shape, F32), dma((2, 4)),
        ],
        compiler_params=pltpu.CompilerParams(vmem_limit_bytes=62 * 1024 * 1024),
        name="hand_on",
    )(adjoint, siting_gradient)
    return jnp.transpose(adjoint, (1, 0, 2)), siting_gradient


def solution(mesh):
    placed = (
        P("scen", "tm", None),
        P("tm", None, None, None),
        P(),
        P(),
        P("tm", None, None),
        P("tm"),
        P("scen"),
    )
    return jax.shard_map(
        functools.partial(per_device, mesh.shape["tm"], mesh.shape["scen"]),
        mesh=mesh,
        in_specs=placed,
        out_specs=(P("scen", "tm", None), P("tm", "scen")),
        check_vma=False,
    )
```

```python
import functools

import jax
import jax.numpy as jnp
from jax import lax
from jax.experimental import pallas as pl
from jax.experimental.pallas import tpu as pltpu
from jax.sharding import PartitionSpec as P

SWEEPS = 2
MESH = pl.DeviceIdType.MESH
F32 = jnp.float32
BF16 = jnp.bfloat16


def kernel(
    tms, scs,
    cot_hbm, blk_hbm, links_ref, step_hbm, coup_hbm, band_ref, cand_hbm,
    out_hbm, sit_hbm,
    cot_ref, step_ref, coup_ref, cand_ref, out_ref, sit_ref, in_sem, out_sem,
    adj, sbuf, recv, tsend, trecv, wall, turned, spread_in, spread_out, gacc, gsum, grecv,
    s_send, s_recv, t_send, t_recv, wz_send, wz_recv, wx_send, wx_recv, wy_send, wy_recv,
    wc_send, wc_recv, g_send, g_recv,
):
    me = lax.axis_index("tm")
    mine = lax.axis_index("scen")
    hours, scens, _ = cot_ref.shape
    zones, rows, bus = adj.shape
    parts, width, depth = wall.shape[:3]
    fan = links_ref.shape[1]
    share = zones // scs
    used = hours * scens
    total = tms * hours
    padded = gsum.shape[1]
    slot = rows // scens
    col = lax.rem(me, width)
    plane = lax.div(me, width)
    by_reach = sorted(range(1, tms), key=lambda o: abs(2 * o - tms))
    turns = [by_reach[i // 2] if i % 2 == 0 else by_reach[-1 - i // 2] for i in range(tms - 1)]
    both_last = (((1,), (1,)), ((), ()))

    loads = [
        pltpu.make_async_copy(src, dst, in_sem.at[i])
        for i, (src, dst) in enumerate([
            (cot_hbm, cot_ref), (step_hbm, step_ref), (blk_hbm.at[mine], wall.at[mine, col, plane]),
            (coup_hbm, coup_ref), (cand_hbm, cand_ref),
        ])
    ]
    for load in loads:
        load.start()
    barrier = pltpu.get_barrier_semaphore()
    for o in range(1, tms):
        pl.semaphore_signal(barrier, inc=1, device_id={"tm": lax.rem(me + o, tms)}, device_id_type=MESH)
    for o in range(1, scs):
        pl.semaphore_signal(barrier, inc=1, device_id={"scen": lax.rem(mine + o, scs)}, device_id_type=MESH)

    def remote(src, dst, send, got, axis, peer):
        copy = pltpu.make_async_remote_copy(
            src_ref=src, dst_ref=dst, send_sem=send, recv_sem=got,
            device_id={axis: peer}, device_id_type=MESH,
        )
        copy.start()
        return copy

    def scale(sweep, z):
        weighted = adj[z] * step_ref[z]
        sbuf[sweep, z] = weighted.astype(BF16)
        gacc[z] = weighted if sweep == 0 else gacc[z] + weighted

    def send_scaled(sweep, o):
        to = lax.rem(me + o, tms)
        return remote(
            sbuf.at[sweep, to], recv.at[sweep, me], s_send.at[sweep, o], s_recv.at[sweep, o], "tm", to
        )

    def temporal(sweep):
        spread_in[...] = recv[sweep].reshape(tms * rows, bus).astype(F32)
        side = jnp.concatenate(
            [spread_in[pl.ds(s, tms * slot, stride=scens), :].astype(BF16) for s in range(scens)], axis=1
        )
        term = jnp.dot(turned[...], side, preferred_element_type=F32)
        for s in range(scens):
            spread_out[pl.ds(s, tms * slot, stride=scens), :] = term[:, s * bus:(s + 1) * bus]
        tsend[sweep] = spread_out[...].reshape(tms, rows, bus).astype(BF16)
        copies = {}
        for o in turns:
            to = lax.rem(me + o, tms)
            copies[o] = remote(
                tsend.at[sweep, to], trecv.at[sweep, me], t_send.at[sweep, o], t_recv.at[sweep, o], "tm", to
            )
        trecv[sweep, me] = tsend[sweep, me]
        return copies

    def network(sweep):
        def one(z, _):
            picked = jnp.concatenate([sbuf[sweep, links_ref[z, k]] for k in range(fan)], axis=1)
            weights = jnp.concatenate(
                [wall[p, lax.rem(z, width), lax.div(z, width)] for p in range(parts)], axis=0
            )
            adj[z] = adj[z] - jnp.dot(picked, weights, preferred_element_type=F32)
            return 0

        lax.fori_loop(0, zones, one, 0, unroll=2)

    loads[0].wait()
    loads[1].wait()
    for z in range(zones):
        adj[z, used // 16 * 16:rows, :] = jnp.zeros((rows - used // 16 * 16, bus), F32)
        adj[z, 0:used, :] = cot_ref[:, :, z * bus:(z + 1) * bus].reshape(used, bus)
        scale(0, z)
    loads[2].wait()
    pl.semaphore_wait(barrier, tms - 1 + scs - 1)

    along_z = []
    for o in range(1, depth):
        to = lax.rem(plane + o, depth) * width + col
        piece = wall.at[mine, col, plane]
        along_z.append(remote(piece, piece, wz_send.at[o], wz_recv.at[o], "tm", to))
    scaled_out = {o: send_scaled(0, o) for o in turns}
    recv[0, me] = sbuf[0, me]

    loads[3].wait()
    loads[4].wait()
    spread = lax.broadcasted_iota(jnp.int32, (total, total), 0) - lax.broadcasted_iota(jnp.int32, (total, total), 1)
    masked = jnp.where(jnp.abs(spread) <= band_ref[0], coup_ref[...].astype(F32), 0.0).astype(BF16)
    wide = lax.broadcasted_iota(jnp.int32, (tms * slot, 1), 0)
    device = jnp.zeros_like(wide)
    for j in range(1, tms):
        device = device + (wide >= j * slot).astype(jnp.int32)
    within = wide - device * slot
    hour = jnp.where(within < hours, device * hours + within, -1)
    pick = jnp.where(hour == lax.broadcasted_iota(jnp.int32, (tms * slot, total), 1), 1.0, 0.0).astype(BF16)
    half = lax.dot_general(pick, masked, both_last, preferred_element_type=F32).astype(BF16)
    turned[...] = lax.dot_general(half, pick, both_last, preferred_element_type=F32).astype(BF16)

    core = lax.rem(mine, 2)
    along_y = {}

    def to_same_core(back):
        held = lax.rem(col + width - back, width)
        for o in range(1, scs // 2):
            piece = wall.at[mine, held]
            along_y[o, back] = remote(
                piece, piece, wy_send.at[o, back], wy_recv.at[o, back], "scen", lax.rem(mine + 2 * o, scs)
            )

    for copy in along_z:
        copy.wait_recv()
    along_x = []
    for o in range(1, width):
        piece = wall.at[mine, col]
        to = plane * width + lax.rem(col + o, width)
        along_x.append(remote(piece, piece, wx_send.at[o], wx_recv.at[o], "tm", to))
    to_same_core(0)
    for o in range(1, width):
        along_x[o - 1].wait_recv()
        to_same_core(o)
    piece = wall.at[mine]
    to_core = [remote(piece, piece, wc_send.at[0], wc_recv.at[0], "scen", mine + 1 - 2 * core)]

    for o in turns:
        scaled_out[o].wait_recv()
    temporal_out = temporal(0)
    sent = along_z + along_x + list(along_y.values()) + list(scaled_out.values()) + list(temporal_out.values())

    for o in range(1, scs // 2):
        for back in range(width):
            along_y[o, back].wait_recv()
        piece = wall.at[lax.rem(mine + scs - 2 * o, scs)]
        to_core.append(remote(piece, piece, wc_send.at[o], wc_recv.at[o], "scen", mine + 1 - 2 * core))
    for copy in to_core:
        copy.wait_recv()
    sent += to_core

    network(0)
    scaled_out = {}
    for o in [tms - o for o in turns]:
        zone = lax.rem(me + o, tms)
        temporal_out[tms - o].wait_recv()
        adj[zone] = adj[zone] - trecv[0, zone].astype(F32)
        scale(1, zone)
        scaled_out[o] = send_scaled(1, o)
    adj[me] = adj[me] - trecv[0, me].astype(F32)
    scale(1, me)
    recv[1, me] = sbuf[1, me]

    network(1)

    hour_of = lax.broadcasted_iota(jnp.int32, (padded, rows), 1) - scens * lax.broadcasted_iota(
        jnp.int32, (padded, rows), 0
    )
    fold = jnp.where((hour_of >= 0) & (hour_of < scens), 1.0 / (scens * scs), 0.0)

    def fold_zone(z, _):
        gsum[z] = jnp.dot(fold, gacc[z], preferred_element_type=F32, precision=lax.Precision.HIGHEST)
        return 0

    lax.fori_loop(0, zones, fold_zone, 0)
    grads = []
    for o in range(1, scs):
        peer = lax.rem(mine + o, scs)
        grads.append(remote(
            gsum.at[pl.ds(peer * share, share)], grecv.at[o], g_send.at[o], g_recv.at[o], "scen", peer
        ))

    for o in turns:
        scaled_out[o].wait_recv()
    temporal_out = temporal(1)
    sent += list(scaled_out.values()) + list(temporal_out.values()) + grads

    for copy in grads:
        copy.wait_recv()
    summed = gsum[pl.ds(mine * share, share)]
    for o in range(1, scs):
        summed = summed + grecv[o]
    local = cand_ref[...] - mine * (share * bus)
    siting = jnp.zeros((padded, cand_ref.shape[1]), F32)
    for part in range(share):
        ids = lax.broadcasted_iota(jnp.int32, (bus, cand_ref.shape[1]), 0) + part * bus
        chosen = jnp.where(ids == local, 1.0, 0.0)
        siting = siting + jnp.dot(
            summed[part], chosen, preferred_element_type=F32, precision=lax.Precision.HIGHEST
        )
    sit_ref[...] = siting[0:hours]
    stores = [pltpu.make_async_copy(sit_ref, sit_hbm, out_sem.at[0])]
    stores[0].start()

    def finish(zone, o):
        value = adj[zone] - trecv[1, zone].astype(F32)
        lanes = pl.ds(pl.multiple_of(zone * bus, bus), bus)
        out_ref[:, :, lanes] = value[0:used].reshape(hours, scens, bus)
        store = pltpu.make_async_copy(out_ref.at[:, :, lanes], out_hbm.at[:, :, lanes], out_sem.at[o + 1])
        store.start()
        stores.append(store)

    finish(me, 0)
    for o in [tms - o for o in turns]:
        temporal_out[tms - o].wait_recv()
        finish(lax.rem(me + o, tms), o)
    for copy in sent:
        copy.wait_send()
    for store in stores:
        store.wait()


def hand_on(adj_in, sit_in, adj_out, sit_out, adj, sit, sem):
    hours = adj_in.shape[0]
    cuts = 3 if hours % 3 == 0 else 1
    step = hours // cuts
    spans = [pl.ds(i * step, step) for i in range(cuts)]
    legs = [(sit_in, sit, sit_out)] + [(adj_in.at[at], adj.at[at], adj_out.at[at]) for at in spans]
    inward = [pltpu.make_async_copy(src, mid, sem.at[0, i]) for i, (src, mid, _) in enumerate(legs)]
    outward = [pltpu.make_async_copy(mid, dst, sem.at[1, i]) for i, (_, mid, dst) in enumerate(legs)]
    for copy in inward:
        copy.start()
    for first, second in zip(inward, outward):
        first.wait()
        second.start()
    for copy in outward:
        copy.wait()


def per_device(tms, scs, cotangent, blocks, zone_links, step_size, coupling, ramp_band, candidates):
    scens, hours, buses = cotangent.shape
    _, fan, bus, _ = blocks.shape
    zones = buses // bus
    rows = -(-hours * scens // 16) * 16
    padded = -(-hours // 8) * 8
    cut = fan * bus // scs
    width = 1
    while 4 * width * width <= tms:
        width *= 2
    depth = tms // width
    hbm = pl.BlockSpec(memory_space=pltpu.HBM)
    smem = pl.BlockSpec(memory_space=pltpu.SMEM)
    dma = pltpu.SemaphoreType.DMA
    adjoint, siting_gradient = pl.pallas_call(
        functools.partial(kernel, tms, scs),
        out_shape=(
            jax.ShapeDtypeStruct((hours, scens, buses), F32),
            jax.ShapeDtypeStruct((hours, candidates.shape[0]), F32),
        ),
        in_specs=[hbm, hbm, smem, hbm, hbm, smem, hbm],
        out_specs=(hbm, hbm),
        scratch_shapes=[
            pltpu.VMEM((hours, scens, buses), F32),
            pltpu.VMEM((zones, 1, bus), F32),
            pltpu.VMEM(coupling.shape[1:], BF16),
            pltpu.VMEM((1, candidates.shape[0]), jnp.int32),
            pltpu.VMEM((hours, scens, buses), F32),
            pltpu.VMEM((hours, candidates.shape[0]), F32),
            dma((5,)), dma((tms + 1,)),
            pltpu.VMEM((zones, rows, bus), F32),
            pltpu.VMEM((SWEEPS, zones, rows, bus), BF16),
            pltpu.VMEM((SWEEPS, tms, rows, bus), BF16),
            pltpu.VMEM((SWEEPS, tms, rows, bus), BF16),
            pltpu.VMEM((SWEEPS, zones, rows, bus), BF16),
            pltpu.VMEM((scs, width, depth, cut, bus), BF16),
            pltpu.VMEM((tms * (rows // scens), tms * (rows // scens)), BF16),
            pltpu.VMEM((tms * rows, bus), F32),
            pltpu.VMEM((tms * rows, bus), F32),
            pltpu.VMEM((zones, rows, bus), F32),
            pltpu.VMEM((zones, padded, bus), F32),
            pltpu.VMEM((scs, zones // scs, padded, bus), F32),
            dma((SWEEPS, tms)), dma((SWEEPS, tms)), dma((SWEEPS, tms)), dma((SWEEPS, tms)),
            dma((depth,)), dma((depth,)), dma((width,)), dma((width,)),
            dma((scs, width)), dma((scs, width)), dma((scs,)), dma((scs,)), dma((scs,)), dma((scs,)),
        ],
        compiler_params=pltpu.CompilerParams(
            collective_id=0, has_side_effects=True, vmem_limit_bytes=62 * 1024 * 1024
        ),
        name="sweeps",
    )(
        jnp.transpose(cotangent, (1, 0, 2)),
        blocks.reshape(scs, cut, bus),
        zone_links,
        step_size.reshape(zones, 1, bus),
        coupling.reshape(coupling.shape[1:]),
        ramp_band,
        candidates.reshape(1, -1),
    )
    adjoint, siting_gradient = pl.pallas_call(
        hand_on,
        out_shape=(
            jax.ShapeDtypeStruct(adjoint.shape, F32),
            jax.ShapeDtypeStruct(siting_gradient.shape, F32),
        ),
        in_specs=[hbm, hbm],
        out_specs=(hbm, hbm),
        scratch_shapes=[
            pltpu.VMEM(adjoint.shape, F32), pltpu.VMEM(siting_gradient.shape, F32), dma((2, 4)),
        ],
        compiler_params=pltpu.CompilerParams(vmem_limit_bytes=62 * 1024 * 1024),
        name="hand_on",
    )(adjoint, siting_gradient)
    return jnp.transpose(adjoint, (1, 0, 2)), siting_gradient


def solution(mesh):
    placed = (
        P("scen", "tm", None),
        P("tm", None, None, None),
        P(),
        P(),
        P("tm", None, None),
        P("tm"),
        P("scen"),
    )
    return jax.shard_map(
        functools.partial(per_device, mesh.shape["tm"], mesh.shape["scen"]),
        mesh=mesh,
        in_specs=placed,
        out_specs=(P("scen", "tm", None), P("tm", "scen")),
        check_vma=False,
    )
```

```python
import functools

import jax
import jax.numpy as jnp
from jax import lax
from jax.experimental import pallas as pl
from jax.experimental.pallas import tpu as pltpu
from jax.sharding import PartitionSpec as P

SWEEPS = 2
MESH = pl.DeviceIdType.MESH
F32 = jnp.float32
BF16 = jnp.bfloat16


def kernel(
    tms, scs,
    cot_hbm, blk_hbm, links_ref, step_hbm, coup_hbm, band_ref, cand_hbm,
    out_hbm, sit_hbm,
    cot_ref, step_ref, coup_ref, cand_ref, out_ref, sit_ref, in_sem, out_sem,
    adj, sbuf, recv, tsend, trecv, wall, turned, spread_in, spread_out, gacc, gsum, grecv,
    s_send, s_recv, t_send, t_recv, wz_send, wz_recv, wx_send, wx_recv, wy_send, wy_recv,
    wc_send, wc_recv, g_send, g_recv,
):
    me = lax.axis_index("tm")
    mine = lax.axis_index("scen")
    hours, scens, _ = cot_ref.shape
    zones, rows, bus = adj.shape
    parts, width, depth = wall.shape[:3]
    fan = links_ref.shape[1]
    share = zones // scs
    used = hours * scens
    total = tms * hours
    padded = gsum.shape[1]
    slot = rows // scens
    col = lax.rem(me, width)
    plane = lax.div(me, width)
    far_first = sorted(range(1, tms), key=lambda o: abs(2 * o - tms))
    both_last = (((1,), (1,)), ((), ()))

    loads = [
        pltpu.make_async_copy(src, dst, in_sem.at[i])
        for i, (src, dst) in enumerate([
            (cot_hbm, cot_ref), (step_hbm, step_ref), (blk_hbm.at[mine], wall.at[mine, col, plane]),
            (coup_hbm, coup_ref), (cand_hbm, cand_ref),
        ])
    ]
    for load in loads:
        load.start()
    barrier = pltpu.get_barrier_semaphore()
    for o in range(1, tms):
        pl.semaphore_signal(barrier, inc=1, device_id={"tm": lax.rem(me + o, tms)}, device_id_type=MESH)
    for o in range(1, scs):
        pl.semaphore_signal(barrier, inc=1, device_id={"scen": lax.rem(mine + o, scs)}, device_id_type=MESH)

    def remote(src, dst, send, got, axis, peer):
        copy = pltpu.make_async_remote_copy(
            src_ref=src, dst_ref=dst, send_sem=send, recv_sem=got,
            device_id={axis: peer}, device_id_type=MESH,
        )
        copy.start()
        return copy

    def scale(sweep, z):
        weighted = adj[z] * step_ref[z]
        sbuf[sweep, z] = weighted.astype(BF16)
        gacc[z] = weighted if sweep == 0 else gacc[z] + weighted

    def send_scaled(sweep, o):
        to = lax.rem(me + o, tms)
        return remote(
            sbuf.at[sweep, to], recv.at[sweep, me], s_send.at[sweep, o], s_recv.at[sweep, o], "tm", to
        )

    def temporal(sweep):
        spread_in[...] = recv[sweep].reshape(tms * rows, bus).astype(F32)
        side = jnp.concatenate(
            [spread_in[pl.ds(s, tms * slot, stride=scens), :].astype(BF16) for s in range(scens)], axis=1
        )
        term = jnp.dot(turned[...], side, preferred_element_type=F32)
        for s in range(scens):
            spread_out[pl.ds(s, tms * slot, stride=scens), :] = term[:, s * bus:(s + 1) * bus]
        tsend[sweep] = spread_out[...].reshape(tms, rows, bus).astype(BF16)
        copies = {}
        for o in far_first:
            to = lax.rem(me + o, tms)
            copies[o] = remote(
                tsend.at[sweep, to], trecv.at[sweep, me], t_send.at[sweep, o], t_recv.at[sweep, o], "tm", to
            )
        trecv[sweep, me] = tsend[sweep, me]
        return copies

    def network(sweep):
        def one(z, _):
            picked = jnp.concatenate([sbuf[sweep, links_ref[z, k]] for k in range(fan)], axis=1)
            weights = jnp.concatenate(
                [wall[p, lax.rem(z, width), lax.div(z, width)] for p in range(parts)], axis=0
            )
            adj[z] = adj[z] - jnp.dot(picked, weights, preferred_element_type=F32)
            return 0

        lax.fori_loop(0, zones, one, 0, unroll=2)

    loads[0].wait()
    loads[1].wait()
    for z in range(zones):
        adj[z, used // 16 * 16:rows, :] = jnp.zeros((rows - used // 16 * 16, bus), F32)
        adj[z, 0:used, :] = cot_ref[:, :, z * bus:(z + 1) * bus].reshape(used, bus)
        scale(0, z)
    loads[2].wait()
    pl.semaphore_wait(barrier, tms - 1 + scs - 1)

    along_z = []
    for o in range(1, depth):
        to = lax.rem(plane + o, depth) * width + col
        piece = wall.at[mine, col, plane]
        along_z.append(remote(piece, piece, wz_send.at[o], wz_recv.at[o], "tm", to))
    scaled_out = {o: send_scaled(0, o) for o in far_first}
    recv[0, me] = sbuf[0, me]

    loads[3].wait()
    loads[4].wait()
    spread = lax.broadcasted_iota(jnp.int32, (total, total), 0) - lax.broadcasted_iota(jnp.int32, (total, total), 1)
    masked = jnp.where(jnp.abs(spread) <= band_ref[0], coup_ref[...].astype(F32), 0.0).astype(BF16)
    wide = lax.broadcasted_iota(jnp.int32, (tms * slot, 1), 0)
    device = jnp.zeros_like(wide)
    for j in range(1, tms):
        device = device + (wide >= j * slot).astype(jnp.int32)
    within = wide - device * slot
    hour = jnp.where(within < hours, device * hours + within, -1)
    pick = jnp.where(hour == lax.broadcasted_iota(jnp.int32, (tms * slot, total), 1), 1.0, 0.0).astype(BF16)
    half = lax.dot_general(pick, masked, both_last, preferred_element_type=F32).astype(BF16)
    turned[...] = lax.dot_general(half, pick, both_last, preferred_element_type=F32).astype(BF16)

    core = lax.rem(mine, 2)
    along_y = {}

    def to_same_core(back):
        held = lax.rem(col + width - back, width)
        for o in range(1, scs // 2):
            piece = wall.at[mine, held]
            along_y[o, back] = remote(
                piece, piece, wy_send.at[o, back], wy_recv.at[o, back], "scen", lax.rem(mine + 2 * o, scs)
            )

    for copy in along_z:
        copy.wait_recv()
    along_x = []
    for o in range(1, width):
        piece = wall.at[mine, col]
        to = plane * width + lax.rem(col + o, width)
        along_x.append(remote(piece, piece, wx_send.at[o], wx_recv.at[o], "tm", to))
    to_same_core(0)

    for o in far_first:
        scaled_out[o].wait_recv()
    temporal_out = temporal(0)
    for o in range(1, width):
        along_x[o - 1].wait_recv()
        to_same_core(o)
    sent = along_z + along_x + list(along_y.values()) + list(scaled_out.values()) + list(temporal_out.values())

    to_core = []
    for o in range(scs // 2):
        if o > 0:
            for back in range(width):
                along_y[o, back].wait_recv()
        piece = wall.at[lax.rem(mine + scs - 2 * o, scs)]
        to_core.append(remote(piece, piece, wc_send.at[o], wc_recv.at[o], "scen", mine + 1 - 2 * core))
    for copy in to_core:
        copy.wait_recv()
    sent += to_core

    network(0)
    scaled_out = {}
    for o in far_first:
        zone = lax.rem(me + o, tms)
        temporal_out[tms - o].wait_recv()
        adj[zone] = adj[zone] - trecv[0, zone].astype(F32)
        scale(1, zone)
        scaled_out[o] = send_scaled(1, o)
    adj[me] = adj[me] - trecv[0, me].astype(F32)
    scale(1, me)
    recv[1, me] = sbuf[1, me]

    network(1)

    hour_of = lax.broadcasted_iota(jnp.int32, (padded, rows), 1) - scens * lax.broadcasted_iota(
        jnp.int32, (padded, rows), 0
    )
    fold = jnp.where((hour_of >= 0) & (hour_of < scens), 1.0 / (scens * scs), 0.0)

    def fold_zone(z, _):
        gsum[z] = jnp.dot(fold, gacc[z], preferred_element_type=F32, precision=lax.Precision.HIGHEST)
        return 0

    lax.fori_loop(0, zones, fold_zone, 0)
    grads = []
    for o in range(1, scs):
        peer = lax.rem(mine + o, scs)
        grads.append(remote(
            gsum.at[pl.ds(peer * share, share)], grecv.at[o], g_send.at[o], g_recv.at[o], "scen", peer
        ))

    for o in far_first:
        scaled_out[o].wait_recv()
    temporal_out = temporal(1)
    sent += list(scaled_out.values()) + list(temporal_out.values()) + grads

    for copy in grads:
        copy.wait_recv()
    summed = gsum[pl.ds(mine * share, share)]
    for o in range(1, scs):
        summed = summed + grecv[o]
    local = cand_ref[...] - mine * (share * bus)
    siting = jnp.zeros((padded, cand_ref.shape[1]), F32)
    for part in range(share):
        ids = lax.broadcasted_iota(jnp.int32, (bus, cand_ref.shape[1]), 0) + part * bus
        chosen = jnp.where(ids == local, 1.0, 0.0)
        siting = siting + jnp.dot(
            summed[part], chosen, preferred_element_type=F32, precision=lax.Precision.HIGHEST
        )
    sit_ref[...] = siting[0:hours]
    stores = [pltpu.make_async_copy(sit_ref, sit_hbm, out_sem.at[0])]
    stores[0].start()

    def finish(zone, o):
        value = adj[zone] - trecv[1, zone].astype(F32)
        lanes = pl.ds(pl.multiple_of(zone * bus, bus), bus)
        out_ref[:, :, lanes] = value[0:used].reshape(hours, scens, bus)
        store = pltpu.make_async_copy(out_ref.at[:, :, lanes], out_hbm.at[:, :, lanes], out_sem.at[o + 1])
        store.start()
        stores.append(store)

    finish(me, 0)
    for o in far_first:
        temporal_out[tms - o].wait_recv()
        finish(lax.rem(me + o, tms), o)
    for copy in sent:
        copy.wait_send()
    for store in stores:
        store.wait()


def hand_on(adj_in, sit_in, adj_out, sit_out, adj, sit, sem):
    hours = adj_in.shape[0]
    cuts = 3 if hours % 3 == 0 else 1
    step = hours // cuts
    spans = [pl.ds(i * step, step) for i in range(cuts)]
    legs = [(sit_in, sit, sit_out)] + [(adj_in.at[at], adj.at[at], adj_out.at[at]) for at in spans]
    inward = [pltpu.make_async_copy(src, mid, sem.at[0, i]) for i, (src, mid, _) in enumerate(legs)]
    outward = [pltpu.make_async_copy(mid, dst, sem.at[1, i]) for i, (_, mid, dst) in enumerate(legs)]
    for copy in inward:
        copy.start()
    for first, second in zip(inward, outward):
        first.wait()
        second.start()
    for copy in outward:
        copy.wait()


def per_device(tms, scs, cotangent, blocks, zone_links, step_size, coupling, ramp_band, candidates):
    scens, hours, buses = cotangent.shape
    _, fan, bus, _ = blocks.shape
    zones = buses // bus
    rows = -(-hours * scens // 16) * 16
    padded = -(-hours // 8) * 8
    cut = fan * bus // scs
    width = 1
    while 4 * width * width <= tms:
        width *= 2
    depth = tms // width
    hbm = pl.BlockSpec(memory_space=pltpu.HBM)
    smem = pl.BlockSpec(memory_space=pltpu.SMEM)
    dma = pltpu.SemaphoreType.DMA
    adjoint, siting_gradient = pl.pallas_call(
        functools.partial(kernel, tms, scs),
        out_shape=(
            jax.ShapeDtypeStruct((hours, scens, buses), F32),
            jax.ShapeDtypeStruct((hours, candidates.shape[0]), F32),
        ),
        in_specs=[hbm, hbm, smem, hbm, hbm, smem, hbm],
        out_specs=(hbm, hbm),
        scratch_shapes=[
            pltpu.VMEM((hours, scens, buses), F32),
            pltpu.VMEM((zones, 1, bus), F32),
            pltpu.VMEM(coupling.shape[1:], BF16),
            pltpu.VMEM((1, candidates.shape[0]), jnp.int32),
            pltpu.VMEM((hours, scens, buses), F32),
            pltpu.VMEM((hours, candidates.shape[0]), F32),
            dma((5,)), dma((tms + 1,)),
            pltpu.VMEM((zones, rows, bus), F32),
            pltpu.VMEM((SWEEPS, zones, rows, bus), BF16),
            pltpu.VMEM((SWEEPS, tms, rows, bus), BF16),
            pltpu.VMEM((SWEEPS, tms, rows, bus), BF16),
            pltpu.VMEM((SWEEPS, zones, rows, bus), BF16),
            pltpu.VMEM((scs, width, depth, cut, bus), BF16),
            pltpu.VMEM((tms * (rows // scens), tms * (rows // scens)), BF16),
            pltpu.VMEM((tms * rows, bus), F32),
            pltpu.VMEM((tms * rows, bus), F32),
            pltpu.VMEM((zones, rows, bus), F32),
            pltpu.VMEM((zones, padded, bus), F32),
            pltpu.VMEM((scs, zones // scs, padded, bus), F32),
            dma((SWEEPS, tms)), dma((SWEEPS, tms)), dma((SWEEPS, tms)), dma((SWEEPS, tms)),
            dma((depth,)), dma((depth,)), dma((width,)), dma((width,)),
            dma((scs, width)), dma((scs, width)), dma((scs,)), dma((scs,)), dma((scs,)), dma((scs,)),
        ],
        compiler_params=pltpu.CompilerParams(
            collective_id=0, has_side_effects=True, vmem_limit_bytes=62 * 1024 * 1024
        ),
        name="sweeps",
    )(
        jnp.transpose(cotangent, (1, 0, 2)),
        blocks.reshape(scs, cut, bus),
        zone_links,
        step_size.reshape(zones, 1, bus),
        coupling.reshape(coupling.shape[1:]),
        ramp_band,
        candidates.reshape(1, -1),
    )
    adjoint, siting_gradient = pl.pallas_call(
        hand_on,
        out_shape=(
            jax.ShapeDtypeStruct(adjoint.shape, F32),
            jax.ShapeDtypeStruct(siting_gradient.shape, F32),
        ),
        in_specs=[hbm, hbm],
        out_specs=(hbm, hbm),
        scratch_shapes=[
            pltpu.VMEM(adjoint.shape, F32), pltpu.VMEM(siting_gradient.shape, F32), dma((2, 4)),
        ],
        compiler_params=pltpu.CompilerParams(vmem_limit_bytes=62 * 1024 * 1024),
        name="hand_on",
    )(adjoint, siting_gradient)
    return jnp.transpose(adjoint, (1, 0, 2)), siting_gradient


def solution(mesh):
    placed = (
        P("scen", "tm", None),
        P("tm", None, None, None),
        P(),
        P(),
        P("tm", None, None),
        P("tm"),
        P("scen"),
    )
    return jax.shard_map(
        functools.partial(per_device, mesh.shape["tm"], mesh.shape["scen"]),
        mesh=mesh,
        in_specs=placed,
        out_specs=(P("scen", "tm", None), P("tm", "scen")),
        check_vma=False,
    )
```
